512 devices in a mesh: blk: 32 (over z, y_lo), col: 16 (over x, y_hi, core).
Axes of the slice: x: 4, y: 4 (y_hi: 2, y_lo: 2; y = y_hi * 2 + y_lo), z: 16, core: 2. Of those that a mesh axis runs over, the one named last changes fastest.
Arguments:
- iterate: float32 [4096, 18432], P('blk', 'col'), may hold values from -6 to 6
Outputs:
- updated: float32 [4096, 18432], P('blk', 'col')
The draws below stay inside these ranges and needn't reach their ends.
All inputs are finite; a program needn't handle non-finite values.
Results may differ from the reference program's by a relative error of at most 0.012.
The reference program's roundings to bfloat16 on the way (of `rounded`, `gram_low` and `poly`) count: a program that leaves them out, or rounds other values in their place, can miss the bound.
Values may be sent and summed in bfloat16 or wider, within the bound.
No kernel may reach another device: no remote copies, remote signals or barrier semaphores. Data moves between devices by JAX's collectives and lax.ppermute only.
A program may use at most 64 MiB of HBM per device.

```python
import jax
import jax.numpy as jnp

M = 4096
N = 18432


def block_levels(rng, shape, pieces, smallest, largest):
    gain = 1.0
    for dim, shards_of in pieces:
        heights = jax.random.uniform(jax.random.fold_in(jax.random.fold_in(rng, 6), dim), (shards_of,), jnp.float32, smallest / len(pieces), largest / len(pieces))
        gain = gain * jnp.repeat(jnp.exp(heights), shape[dim] // shards_of).reshape((-1,) + (1,) * (len(shape) - 1 - dim))
    return gain


def centred(own_key, extent, spread, reach, cuts=(), dtype=jnp.bfloat16):
    drawn = jax.random.normal(own_key, extent, jnp.float32) * spread
    if len(cuts) > 0:
        drawn = block_levels(own_key, extent, cuts, -0.22, 0.18) * drawn
    return jnp.clip(drawn, min=-reach, max=reach).astype(dtype)


def setup_inputs(seed: int = 0) -> dict:
    arg_keys = jax.random.split(jax.random.key(seed), 2)
    return {
        "iterate": centred(arg_keys[0], (M, N), 1.0, 6.0, ((0, 32), (1, 16)), jnp.float32),
    }


def reference(iterate):
    rounded = iterate.astype(jnp.bfloat16)
    gram = jnp.dot(rounded, rounded.T, preferred_element_type=jnp.float32) / N
    gram_low = gram.astype(jnp.bfloat16)
    square = jnp.dot(gram_low, gram_low, preferred_element_type=jnp.float32)
    poly = (-4.7750 * gram + 2.0315 * square).astype(jnp.bfloat16)
    product = jnp.dot(poly, rounded, preferred_element_type=jnp.float32)
    return 3.4445 * rounded.astype(jnp.float32) + product
```

```python
import jax
import jax.numpy as jnp
from jax import lax
from jax.sharding import Mesh, PartitionSpec as P

PLANE = ("ylo", "x", "yhi")
CORE_SWAP = ((0, 1), (1, 0))
TURN = ((0, 0), (1, 2), (2, 1), (3, 3))


def share(piece, size):
    copies = jnp.broadcast_to(piece[None], (size,) + piece.shape)
    return lax.all_to_all(copies, PLANE, 0, 0)


def nt(left, right):
    return lax.dot_general(
        left, right, (((1,), (1,)), ((), ())), preferred_element_type=jnp.float32
    )


def tn(left, right):
    return lax.dot_general(
        left, right, (((0,), (0,)), ((), ())), preferred_element_type=jnp.float32
    )


def per_device(iterate):
    rounded = iterate.astype(jnp.bfloat16)
    rows, cols = rounded.shape
    slabs = lax.axis_size("z")
    chips = lax.axis_size(PLANE)
    total_cols = cols * chips
    own = lax.ppermute(rounded, ("ylo", "core"), TURN)
    half = lax.all_gather(own, "z", axis=0, tiled=True)
    other = lax.ppermute(own, "core", CORE_SWAP)
    partial_gram = nt(half, jnp.concatenate([own, other], 0))
    partial_gram = partial_gram.reshape(chips, rows, 2 * rows)
    summands = lax.all_to_all(partial_gram, PLANE, 0, 0)
    gram = summands.sum(0) / total_cols
    gram_low = gram.astype(jnp.bfloat16)
    left = lax.all_gather(gram_low, "z", axis=0)
    right_own = share(gram_low, chips)
    right_other = lax.ppermute(right_own, "core", CORE_SWAP)
    right_other = jnp.concatenate(
        [right_other[:, :, rows:], right_other[:, :, :rows]], 2
    )
    square = 0.0
    for place, right in enumerate((right_own, right_other)):
        square = square + lax.dot_general(
            left[:, :, place * rows : (place + 1) * rows],
            right,
            (((0, 2), (0, 1)), ((), ())),
            preferred_element_type=jnp.float32,
        )
    poly = (-4.775 * gram + 2.0315 * square).astype(jnp.bfloat16)
    panel = share(poly, chips).reshape(chips * rows, 2 * rows)
    away = tn(panel[:, rows:], half)
    away = lax.ppermute(away, "core", CORE_SWAP)
    product = tn(panel[:, :rows], half) + away
    product = lax.ppermute(product, ("ylo", "core"), TURN)
    return 3.4445 * rounded.astype(jnp.float32) + product


def solution(mesh):
    fine = Mesh(mesh.devices.reshape(16, 2, 4, 2, 2), ("z", "ylo", "x", "yhi", "core"))
    spec = P(("z", "ylo"), ("x", "yhi", "core"))
    return jax.shard_map(
        per_device, mesh=fine, in_specs=(spec,), out_specs=spec, check_vma=False
    )
```

```python
import jax
import jax.numpy as jnp
from jax import lax
from jax.sharding import Mesh, PartitionSpec as P

AXES = ("zg", "zp", "ylo", "x", "yhi", "core")
SIZES = (8, 2, 2, 4, 2, 2)
LINE = ("zg", "zp")
PLANE = ("ylo", "x", "yhi")
SWAP = ((0, 1), (1, 0))
TURN = ((0, 0), (1, 2), (2, 1), (3, 3))


def share(piece, size):
    copies = jnp.broadcast_to(piece[None], (size,) + piece.shape)
    return lax.all_to_all(copies, PLANE, 0, 0)


def nt(left, right):
    return lax.dot_general(
        left, right, (((1,), (1,)), ((), ())), preferred_element_type=jnp.float32
    )


def tn(left, right):
    return lax.dot_general(
        left, right, (((0,), (0,)), ((), ())), preferred_element_type=jnp.float32
    )


def per_device(iterate):
    rounded = iterate.astype(jnp.bfloat16)
    rows, cols = rounded.shape
    slabs = lax.axis_size(LINE)
    chips = lax.axis_size(PLANE)
    total_cols = cols * chips
    own = lax.ppermute(rounded, ("ylo", "core"), TURN)
    half = lax.all_gather(own, LINE, axis=0, tiled=True)
    other = lax.ppermute(own, "core", SWAP)
    partial_gram = nt(half, jnp.concatenate([own, other], 0))
    partial_gram = partial_gram.reshape(chips, rows, 2 * rows)
    summands = lax.all_to_all(partial_gram, PLANE, 0, 0)
    gram = summands.sum(0) / total_cols
    gram_low = gram.astype(jnp.bfloat16)
    same = lax.all_gather(gram_low, "zg", axis=0)
    cross = lax.ppermute(same, "zp", SWAP)
    gram_after, _ = lax.optimization_barrier((gram_low, same))
    right_own = share(gram_after, chips)
    right_other = lax.ppermute(right_own, "core", SWAP)
    right_other = jnp.concatenate(
        [right_other[:, :, rows:], right_other[:, :, :rows]], 2
    )
    even = lax.axis_index("zp") == 0
    left = jnp.stack(
        [jnp.where(even, same, cross), jnp.where(even, cross, same)], 1
    ).reshape(slabs, rows, 2 * rows)
    square = 0.0
    for place, right in enumerate((right_own, right_other)):
        square = square + lax.dot_general(
            left[:, :, place * rows : (place + 1) * rows],
            right,
            (((0, 2), (0, 1)), ((), ())),
            preferred_element_type=jnp.float32,
        )
    poly = (-4.775 * gram + 2.0315 * square).astype(jnp.bfloat16)
    panel = share(poly, chips).reshape(chips * rows, 2 * rows)
    away = tn(panel[:, rows:], half)
    away = lax.ppermute(away, "core", SWAP)
    product = tn(panel[:, :rows], half) + away
    product = lax.ppermute(product, ("ylo", "core"), TURN)
    return 3.4445 * lax.reduce_precision(iterate, 8, 7) + product


def solution(mesh):
    fine = Mesh(mesh.devices.reshape(SIZES), AXES)
    spec = P(("zg", "zp", "ylo"), ("x", "yhi", "core"))
    return jax.shard_map(
        per_device, mesh=fine, in_specs=(spec,), out_specs=spec, check_vma=False
    )
```

```python
import jax
import jax.numpy as jnp
from jax import lax
from jax.sharding import Mesh, PartitionSpec as P

AXES = ("zg", "zp", "ylo", "x", "yhi", "core")
SIZES = (8, 2, 2, 4, 2, 2)
LINE = ("zg", "zp")
PLANE = ("ylo", "x", "yhi")
SWAP = ((0, 1), (1, 0))
TURN = ((0, 0), (1, 2), (2, 1), (3, 3))
CROSS = ((0, 2), (1, 0), (2, 3), (3, 1))


def share(piece, size):
    copies = jnp.broadcast_to(piece[None], (size,) + piece.shape)
    return lax.all_to_all(copies, PLANE, 0, 0)


def nt(left, right):
    return lax.dot_general(
        left, right, (((1,), (1,)), ((), ())), preferred_element_type=jnp.float32
    )


def tn(left, right):
    return lax.dot_general(
        left, right, (((0,), (0,)), ((), ())), preferred_element_type=jnp.float32
    )


def per_device(iterate):
    rounded = iterate.astype(jnp.bfloat16)
    rows, cols = rounded.shape
    slabs = lax.axis_size(LINE)
    chips = lax.axis_size(PLANE)
    total_cols = cols * chips
    own = lax.ppermute(rounded, ("ylo", "core"), TURN)
    half = lax.all_gather(own, LINE, axis=0, tiled=True)
    other = lax.ppermute(own, "core", SWAP)
    partial_gram = nt(half, jnp.concatenate([own, other], 0))
    partial_gram = partial_gram.reshape(chips, rows, 2 * rows)
    summands = lax.all_to_all(partial_gram, PLANE, 0, 0)
    gram = summands.sum(0) / total_cols
    gram_low = gram.astype(jnp.bfloat16)
    same = lax.all_gather(gram_low, "zg", axis=0)
    cross = lax.ppermute(same, "zp", SWAP)
    gram_after, _ = lax.optimization_barrier((gram_low, same))
    right_own = share(gram_after, chips)
    right_other = lax.ppermute(right_own, "core", SWAP)
    right_other = jnp.concatenate(
        [right_other[:, :, rows:], right_other[:, :, :rows]], 2
    )
    even = lax.axis_index("zp") == 0
    left = jnp.stack(
        [jnp.where(even, same, cross), jnp.where(even, cross, same)], 1
    ).reshape(slabs, rows, 2 * rows)
    square = 0.0
    for place, right in enumerate((right_own, right_other)):
        square = square + lax.dot_general(
            left[:, :, place * rows : (place + 1) * rows],
            right,
            (((0, 2), (0, 1)), ((), ())),
            preferred_element_type=jnp.float32,
        )
    poly = (-4.775 * gram + 2.0315 * square).astype(jnp.bfloat16)
    panel = share(poly, chips).reshape(chips * rows, 2 * rows)
    away = tn(panel[:, rows:], half).astype(jnp.bfloat16)
    away = lax.ppermute(away, ("ylo", "core"), CROSS)
    stay = tn(panel[:, :rows], half) + 3.4445 * own.astype(jnp.float32)
    stay = lax.ppermute(stay.astype(jnp.bfloat16), ("ylo", "core"), TURN)
    return stay.astype(jnp.float32) + away.astype(jnp.float32)


def solution(mesh):
    fine = Mesh(mesh.devices.reshape(SIZES), AXES)
    spec = P(("zg", "zp", "ylo"), ("x", "yhi", "core"))
    return jax.shard_map(
        per_device, mesh=fine, in_specs=(spec,), out_specs=spec, check_vma=False
    )
```

```python
import jax
import jax.numpy as jnp
from jax import lax
from jax.sharding import Mesh, PartitionSpec as P

AXES = ("zh", "zl", "ylo", "x", "yhi", "core")
SIZES = (4, 4, 2, 4, 2, 2)
LINE = ("zh", "zl")
PLANE = ("ylo", "x", "yhi")
SWAP = ((0, 1), (1, 0))
TURN = ((0, 0), (1, 2), (2, 1), (3, 3))
CROSS = ((0, 2), (1, 0), (2, 3), (3, 1))


def share(piece, size):
    copies = jnp.broadcast_to(piece[None], (size,) + piece.shape)
    return lax.all_to_all(copies, PLANE, 0, 0)


def along(piece, shift):
    size = lax.axis_size(LINE)
    pairs = [(place, (place + shift) % size) for place in range(size)]
    return lax.ppermute(piece, LINE, pairs)


def mix(left, right):
    return lax.dot_general(
        left, right, (((0, 2), (0, 1)), ((), ())), preferred_element_type=jnp.float32
    )


def per_device(iterate):
    rounded = iterate.astype(jnp.bfloat16)
    rows, cols = rounded.shape
    groups, steps = lax.axis_size("zh"), lax.axis_size("zl")
    chips = lax.axis_size(PLANE)
    total_cols = cols * chips
    own = lax.ppermute(rounded, ("ylo", "core"), TURN)
    half = lax.all_gather(own, LINE, axis=0)
    other = lax.ppermute(own, "core", SWAP)
    partial_gram = lax.dot_general(
        jnp.concatenate([own, other], 0),
        half,
        (((1,), (2,)), ((), ())),
        preferred_element_type=jnp.float32,
    )
    partial_gram = partial_gram.transpose(1, 0, 2)
    summands = lax.all_to_all(partial_gram, PLANE, 0, 0)
    gram = summands.sum(0) / total_cols
    gram_low = gram.astype(jnp.bfloat16)
    panel = share(gram_low, chips).reshape(groups, steps, 2 * rows, rows)
    here = lax.all_gather(gram_low, "zh", axis=0)
    panel, _ = lax.optimization_barrier((panel, here))
    cut = groups // 2
    right = (
        here,
        along(here, -1),
        along(here, 1),
        jnp.concatenate([along(here[:cut], -2), along(here[cut:], 2)], 0),
    )
    residue = lax.axis_index("zl")
    left_own = [
        lax.dynamic_index_in_dim(panel, (residue + shift) % steps, 1, False)
        for shift in (0, 1, steps - 1, 2)
    ]
    left_other = lax.ppermute(jnp.stack(left_own), "core", SWAP)
    left_other = jnp.concatenate(
        [left_other[:, :, rows:], left_other[:, :, :rows]], 2
    )
    square = 0.0
    for place in range(steps):
        square = square + mix(left_own[place], right[place][:, :rows])
    for place in range(steps):
        square = square + mix(left_other[place], right[place][:, rows:])
    poly = (-4.775 * gram + 2.0315 * square).astype(jnp.bfloat16)
    panel = share(poly, chips)
    away = mix(panel[:, rows:], half).astype(jnp.bfloat16)
    away = lax.ppermute(away, ("ylo", "core"), CROSS)
    stay = mix(panel[:, :rows], half) + 3.4445 * own.astype(jnp.float32)
    stay = lax.ppermute(stay.astype(jnp.bfloat16), ("ylo", "core"), TURN)
    return stay.astype(jnp.float32) + away.astype(jnp.float32)


def solution(mesh):
    fine = Mesh(mesh.devices.reshape(SIZES), AXES)
    spec = P(("zh", "zl", "ylo"), ("x", "yhi", "core"))
    return jax.shard_map(
        per_device, mesh=fine, in_specs=(spec,), out_specs=spec, check_vma=False
    )
```

```python
import jax
import jax.numpy as jnp
from jax import lax
from jax.sharding import Mesh, PartitionSpec as P

AXES = ("zh", "zl", "ylo", "x", "yhi", "core")
SIZES = (4, 4, 2, 4, 2, 2)
LINE = ("zh", "zl")
PLANE = ("ylo", "x", "yhi")
SWAP = ((0, 1), (1, 0))
TURN = ((0, 0), (1, 2), (2, 1), (3, 3))
CROSS = ((0, 2), (1, 0), (2, 3), (3, 1))


def share(piece, size):
    copies = jnp.broadcast_to(piece[None], (size,) + piece.shape)
    return lax.all_to_all(copies, PLANE, 0, 0)


def along(piece, shift):
    size = lax.axis_size(LINE)
    pairs = [(place, (place + shift) % size) for place in range(size)]
    return lax.ppermute(piece, LINE, pairs)


def onward(piece):
    size = lax.axis_size(LINE)
    pairs = [
        (2 * place + core, 2 * ((place + 1 - 2 * core) % size) + core)
        for place in range(size)
        for core in range(2)
    ]
    return lax.ppermute(piece, LINE + ("core",), pairs)


def swap(pieces):
    return list(lax.ppermute(jnp.stack(pieces), "core", SWAP))


def mix(left, right):
    return lax.dot_general(
        left, right, (((0, 2), (0, 1)), ((), ())), preferred_element_type=jnp.float32
    )


def nt(left, right):
    return lax.dot_general(
        left, right, (((1,), (1,)), ((), ())), preferred_element_type=jnp.float32
    )


def tn(left, right):
    return lax.dot_general(
        left, right, (((0,), (0,)), ((), ())), preferred_element_type=jnp.float32
    )


def turn_to(blocks, start):
    size = blocks.shape[0]
    return lax.dynamic_slice_in_dim(
        jnp.concatenate([blocks, blocks], 0), start % size, size, 0
    )


def plane_sum(blocks, both, chips):
    parts = jnp.stack([nt(block, both) for block in blocks])
    parts = parts.reshape(len(blocks), chips, -1, parts.shape[-1])
    return lax.all_to_all(parts.transpose(1, 0, 2, 3), PLANE, 0, 0).sum(0)


def per_device(iterate):
    rounded = iterate.astype(jnp.bfloat16)
    rows, cols = rounded.shape
    groups, steps = lax.axis_size("zh"), lax.axis_size("zl")
    slabs = groups * steps
    chips = lax.axis_size(PLANE)
    total_cols = cols * chips
    slab, core = lax.axis_index(LINE), lax.axis_index("core")
    own = lax.ppermute(rounded, ("ylo", "core"), TURN)
    other = lax.ppermute(own, "core", SWAP)
    both = jnp.concatenate([own, other], 0)
    near, far = [own], [other]
    for step in range(1, slabs // 2):
        near.append(onward(near[-1]))
        far.append(onward(far[-1]))
    near.append(onward(near[-1]))
    back = [None]
    for first, last in ((1, 4), (4, 6), (6, 8)):
        back.extend(swap(far[first:last]))
    order = near[::-1] + back[1:]
    early = plane_sum(order[3:14], both, chips)
    late = plane_sum(order[:3] + order[14:], both, chips)
    gram = jnp.concatenate([late[:3], early, late[3:]], 0) / total_cols
    gram = jnp.where(core == 0, gram, gram[::-1])
    gram = turn_to(gram, slabs + slabs // 2 - core - slab)
    gram_low = gram.astype(jnp.bfloat16)
    gram, gram_low = gram.reshape(rows, 2 * rows), gram_low.reshape(rows, 2 * rows)
    panel = share(gram_low, chips).reshape(chips, slabs, rows // chips, 2 * rows)
    panel = panel.transpose(1, 0, 2, 3).reshape(groups, steps, rows, 2 * rows)
    here = lax.all_gather(gram_low, "zh", axis=0)
    panel, _ = lax.optimization_barrier((panel, here))
    cut = groups // 2
    left = (
        here,
        along(here, -1),
        along(here, 1),
        jnp.concatenate([along(here[:cut], -2), along(here[cut:], 2)], 0),
    )
    residue = lax.axis_index("zl")
    right_own = [
        lax.dynamic_index_in_dim(panel, (residue + shift) % steps, 1, False)
        for shift in (0, 1, steps - 1, 2)
    ]
    right_other = lax.ppermute(jnp.stack(right_own), "core", SWAP)
    right_other = jnp.concatenate(
        [right_other[:, :, :, rows:], right_other[:, :, :, :rows]], 3
    )
    square = 0.0
    for place in range(steps):
        square = square + mix(left[place][:, :, :rows], right_own[place])
    for place in range(steps):
        square = square + mix(left[place][:, :, rows:], right_other[place])
    poly = (-4.775 * gram + 2.0315 * square).astype(jnp.bfloat16)
    poly = poly.reshape(slabs, rows // chips, 2 * rows)
    poly = turn_to(poly, slabs // 2 + slab + core)
    poly = jnp.where(core == 0, poly, poly[::-1])
    panel = share(poly, chips).transpose(1, 0, 2, 3).reshape(slabs * rows, 2 * rows)
    half = jnp.concatenate(order, 0)
    away = tn(panel[:, rows:], half).astype(jnp.bfloat16)
    away = lax.ppermute(away, ("ylo", "core"), CROSS)
    stay = tn(panel[:, :rows], half) + 3.4445 * own.astype(jnp.float32)
    stay = lax.ppermute(stay.astype(jnp.bfloat16), ("ylo", "core"), TURN)
    return stay.astype(jnp.float32) + away.astype(jnp.float32)


def solution(mesh):
    fine = Mesh(mesh.devices.reshape(SIZES), AXES)
    spec = P(("zh", "zl", "ylo"), ("x", "yhi", "core"))
    return jax.shard_map(
        per_device, mesh=fine, in_specs=(spec,), out_specs=spec, check_vma=False
    )
```

```python
import jax
import jax.numpy as jnp
from jax import lax
from jax.sharding import Mesh, PartitionSpec as P

AXES = ("zh", "zl", "ylo", "x", "yhi", "core")
SIZES = (4, 4, 2, 4, 2, 2)
LINE = ("zh", "zl")
PLANE = ("ylo", "x", "yhi")
SWAP = ((0, 1), (1, 0))
TURN = ((0, 0), (1, 2), (2, 1), (3, 3))
CROSS = ((0, 2), (1, 0), (2, 3), (3, 1))


def share(piece, size):
    copies = jnp.broadcast_to(piece[None], (size,) + piece.shape)
    return lax.all_to_all(copies, PLANE, 0, 0)


def along(piece, shift):
    size = lax.axis_size(LINE)
    pairs = [(place, (place + shift) % size) for place in range(size)]
    return lax.ppermute(piece, LINE, pairs)


def onward(piece):
    size = lax.axis_size(LINE)
    pairs = [
        (2 * place + core, 2 * ((place + 1 - 2 * core) % size) + core)
        for place in range(size)
        for core in range(2)
    ]
    return lax.ppermute(piece, LINE + ("core",), pairs)


def swap(pieces):
    return list(lax.ppermute(jnp.stack(pieces), "core", SWAP))


def mix(left, right):
    return lax.dot_general(
        left, right, (((0, 2), (0, 1)), ((), ())), preferred_element_type=jnp.float32
    )


def nt(left, right):
    return lax.dot_general(
        left, right, (((1,), (1,)), ((), ())), preferred_element_type=jnp.float32
    )


def tn(left, right):
    return lax.dot_general(
        left, right, (((0,), (0,)), ((), ())), preferred_element_type=jnp.float32
    )


def turn_to(blocks, start):
    size = blocks.shape[0]
    return lax.dynamic_slice_in_dim(
        jnp.concatenate([blocks, blocks], 0), start % size, size, 0
    )


def products(blocks, both, chips):
    parts = [nt(block, both).reshape(chips, -1, both.shape[0]) for block in blocks]
    return jnp.stack(parts, 1)


def plane_sum(parts):
    return lax.all_to_all(parts, PLANE, 0, 0).sum(0)


def per_device(iterate):
    rounded = iterate.astype(jnp.bfloat16)
    rows, cols = rounded.shape
    groups, steps = lax.axis_size("zh"), lax.axis_size("zl")
    slabs = groups * steps
    chips = lax.axis_size(PLANE)
    total_cols = cols * chips
    slab, core = lax.axis_index(LINE), lax.axis_index("core")
    own = lax.ppermute(rounded, ("ylo", "core"), TURN)
    other = lax.ppermute(own, "core", SWAP)
    both = jnp.concatenate([own, other], 0)
    near, far, back, early = [own], [other], [None], None
    for step in range(1, slabs // 2 + 1):
        near.append(onward(near[-1]))
        if step < slabs // 2:
            far.append(onward(far[-1]))
        if step in (3, 5, 7):
            back.extend(swap(far[len(back) : step + 1]))
        if step in (4, 6):
            *back[1:], near[step] = lax.optimization_barrier(
                tuple(back[1:]) + (near[step],)
            )
        if step == 7:
            early = products(near[5:0:-1] + near[:1] + back[1:6], both, chips)
            early, near[step] = lax.optimization_barrier((early, near[step]))
            early = plane_sum(early)
    order = near[::-1] + back[1:]
    late = products(order[:3] + order[14:], both, chips)
    early, late = lax.optimization_barrier((early, late))
    late = plane_sum(late)
    gram = jnp.concatenate([late[:3], early, late[3:]], 0) / total_cols
    gram = jnp.where(core == 0, gram, gram[::-1])
    gram = turn_to(gram, slabs + slabs // 2 - core - slab)
    gram_low = gram.astype(jnp.bfloat16)
    gram, gram_low = gram.reshape(rows, 2 * rows), gram_low.reshape(rows, 2 * rows)
    panel = share(gram_low, chips).reshape(chips, slabs, rows // chips, 2 * rows)
    panel = panel.transpose(1, 0, 2, 3).reshape(groups, steps, rows, 2 * rows)
    here = lax.all_gather(gram_low, "zh", axis=0)
    panel, _ = lax.optimization_barrier((panel, here))
    cut = groups // 2
    left = (
        here,
        along(here, -1),
        along(here, 1),
        jnp.concatenate([along(here[:cut], -2), along(here[cut:], 2)], 0),
    )
    residue = lax.axis_index("zl")
    right_own = [
        lax.dynamic_index_in_dim(panel, (residue + shift) % steps, 1, False)
        for shift in (0, 1, steps - 1, 2)
    ]
    right_other = lax.ppermute(jnp.stack(right_own), "core", SWAP)
    right_other = jnp.concatenate(
        [right_other[:, :, :, rows:], right_other[:, :, :, :rows]], 3
    )
    square = 0.0
    for place in range(steps):
        square = square + mix(left[place][:, :, :rows], right_own[place])
    for place in range(steps):
        square = square + mix(left[place][:, :, rows:], right_other[place])
    poly = (-4.775 * gram + 2.0315 * square).astype(jnp.bfloat16)
    poly = poly.reshape(slabs, rows // chips, 2 * rows)
    poly = turn_to(poly, slabs // 2 + slab + core)
    poly = jnp.where(core == 0, poly, poly[::-1])
    panel = share(poly, chips).transpose(1, 0, 2, 3).reshape(slabs * rows, 2 * rows)
    half = jnp.concatenate(order, 0)
    away = tn(panel[:, rows:], half).astype(jnp.bfloat16)
    away = lax.ppermute(away, ("ylo", "core"), CROSS)
    stay = tn(panel[:, :rows], half) + 3.4445 * own.astype(jnp.float32)
    stay = lax.ppermute(stay.astype(jnp.bfloat16), ("ylo", "core"), TURN)
    return stay.astype(jnp.float32) + away.astype(jnp.float32)


def solution(mesh):
    fine = Mesh(mesh.devices.reshape(SIZES), AXES)
    spec = P(("zh", "zl", "ylo"), ("x", "yhi", "core"))
    return jax.shard_map(
        per_device, mesh=fine, in_specs=(spec,), out_specs=spec, check_vma=False
    )
```

```python
import jax
import jax.numpy as jnp
from jax import lax
from jax.sharding import Mesh, PartitionSpec as P

AXES = ("zh", "zl", "ylo", "x", "yhi", "core")
SIZES = (4, 4, 2, 4, 2, 2)
LINE = ("zh", "zl")
PLANE = ("ylo", "x", "yhi")
SWAP = ((0, 1), (1, 0))
TURN = ((0, 0), (1, 2), (2, 1), (3, 3))
CROSS = ((0, 2), (1, 0), (2, 3), (3, 1))


def share(piece, size):
    copies = jnp.broadcast_to(piece[None], (size,) + piece.shape)
    return lax.all_to_all(copies, PLANE, 0, 0)


def along(piece, shift):
    size = lax.axis_size(LINE)
    pairs = [(place, (place + shift) % size) for place in range(size)]
    return lax.ppermute(piece, LINE, pairs)


def onward(piece, cores=(0, 1)):
    size = lax.axis_size(LINE)
    pairs = [
        (2 * place + core, 2 * ((place + 1 - 2 * core) % size) + core)
        for place in range(size)
        for core in cores
    ]
    return lax.ppermute(piece, LINE + ("core",), pairs)


def swap(pieces):
    return list(lax.ppermute(jnp.stack(pieces), "core", SWAP))


def mix(left, right):
    return lax.dot_general(
        left, right, (((0, 2), (0, 1)), ((), ())), preferred_element_type=jnp.float32
    )


def nt(left, right):
    return lax.dot_general(
        left, right, (((1,), (1,)), ((), ())), preferred_element_type=jnp.float32
    )


def tn(left, right):
    return lax.dot_general(
        left, right, (((0,), (0,)), ((), ())), preferred_element_type=jnp.float32
    )


def turn_to(blocks, start):
    size = blocks.shape[0]
    return lax.dynamic_slice_in_dim(
        jnp.concatenate([blocks, blocks], 0), start % size, size, 0
    )


def per_device(iterate):
    rounded = iterate.astype(jnp.bfloat16)
    rows, cols = rounded.shape
    groups, steps = lax.axis_size("zh"), lax.axis_size("zl")
    slabs = groups * steps
    chips = lax.axis_size(PLANE)
    total_cols = cols * chips
    slab, core = lax.axis_index(LINE), lax.axis_index("core")
    own = lax.ppermute(rounded, ("ylo", "core"), TURN)
    other = lax.ppermute(own, "core", SWAP)
    both = jnp.concatenate([own, other], 0)
    near, far = [own], [other]
    for step in range(1, slabs // 2):
        near.append(onward(near[-1]))
        far.append(onward(far[-1]))
    near_last, far_last = onward(near[-1], (1,)), onward(far[-1], (1,))
    back = swap(far[1:5]) + swap(far[5:])
    (back_last,) = swap([far_last])
    last = jnp.where(core == 0, back_last, near_last)
    half = jnp.concatenate([last] + near[::-1] + back, 0)
    gram = nt(half, both).reshape(slabs, chips, rows // chips, 2 * rows)
    gram = lax.all_to_all(gram.transpose(1, 0, 2, 3), PLANE, 0, 0).sum(0) / total_cols
    gram = jnp.where(core == 0, gram, gram[::-1])
    gram = turn_to(gram, slabs + slabs // 2 - core - slab)
    gram_low = gram.astype(jnp.bfloat16)
    gram, gram_low = gram.reshape(rows, 2 * rows), gram_low.reshape(rows, 2 * rows)
    panel = share(gram_low, chips).reshape(chips, slabs, rows // chips, 2 * rows)
    panel = panel.transpose(1, 0, 2, 3).reshape(groups, steps, rows, 2 * rows)
    here = lax.all_gather(gram_low, "zh", axis=0)
    panel, _ = lax.optimization_barrier((panel, here))
    cut = groups // 2
    left = (
        here,
        along(here, -1),
        along(here, 1),
        jnp.concatenate([along(here[:cut], -2), along(here[cut:], 2)], 0),
    )
    residue = lax.axis_index("zl")
    right_own = [
        lax.dynamic_index_in_dim(panel, (residue + shift) % steps, 1, False)
        for shift in (0, 1, steps - 1, 2)
    ]
    right_other = lax.ppermute(jnp.stack(right_own), "core", SWAP)
    right_other = jnp.concatenate(
        [right_other[:, :, :, rows:], right_other[:, :, :, :rows]], 3
    )
    square = 0.0
    for place in range(steps):
        square = square + mix(left[place][:, :, :rows], right_own[place])
    for place in range(steps):
        square = square + mix(left[place][:, :, rows:], right_other[place])
    poly = (-4.775 * gram + 2.0315 * square).astype(jnp.bfloat16)
    poly = poly.reshape(slabs, rows // chips, 2 * rows)
    poly = turn_to(poly, slabs // 2 + slab + core)
    poly = jnp.where(core == 0, poly, poly[::-1])
    panel = share(poly, chips).transpose(1, 0, 2, 3).reshape(slabs * rows, 2 * rows)
    away = tn(panel[:, rows:], half).astype(jnp.bfloat16)
    away = lax.ppermute(away, ("ylo", "core"), CROSS)
    stay = tn(panel[:, :rows], half) + 3.4445 * own.astype(jnp.float32)
    stay = lax.ppermute(stay.astype(jnp.bfloat16), ("ylo", "core"), TURN)
    return stay.astype(jnp.float32) + away.astype(jnp.float32)


def solution(mesh):
    fine = Mesh(mesh.devices.reshape(SIZES), AXES)
    spec = P(("zh", "zl", "ylo"), ("x", "yhi", "core"))
    return jax.shard_map(
        per_device, mesh=fine, in_specs=(spec,), out_specs=spec, check_vma=False
    )
```

```python
import jax
import jax.numpy as jnp
from jax import lax
from jax.sharding import Mesh, PartitionSpec as P

AXES = ("zh", "zl", "ylo", "x", "yhi", "core")
SIZES = (4, 4, 2, 4, 2, 2)
LINE = ("zh", "zl")
PLANE = ("ylo", "x", "yhi")
SWAP = ((0, 1), (1, 0))
TURN = ((0, 0), (1, 2), (2, 1), (3, 3))
CROSS = ((0, 2), (1, 0), (2, 3), (3, 1))


def share(piece, size):
    copies = jnp.broadcast_to(piece[None], (size,) + piece.shape)
    return lax.all_to_all(copies, PLANE, 0, 0)


def along(piece, shift):
    size = lax.axis_size(LINE)
    pairs = [(place, (place + shift) % size) for place in range(size)]
    return lax.ppermute(piece, LINE, pairs)


def onward(piece):
    size = lax.axis_size(LINE)
    pairs = [
        (2 * place + core, 2 * ((place + 1 - 2 * core) % size) + core)
        for place in range(size)
        for core in range(2)
    ]
    return lax.ppermute(piece, LINE + ("core",), pairs)


def swap(pieces):
    return list(lax.ppermute(jnp.stack(pieces), "core", SWAP))


def mix(left, right):
    return lax.dot_general(
        left, right, (((0, 2), (0, 1)), ((), ())), preferred_element_type=jnp.float32
    )


def nt(left, right):
    return lax.dot_general(
        left, right, (((1,), (1,)), ((), ())), preferred_element_type=jnp.float32
    )


def tn(left, right):
    return lax.dot_general(
        left, right, (((0,), (0,)), ((), ())), preferred_element_type=jnp.float32
    )


def turn_to(blocks, start):
    size = blocks.shape[0]
    return lax.dynamic_slice_in_dim(
        jnp.concatenate([blocks, blocks], 0), start % size, size, 0
    )


def per_device(iterate):
    rounded = iterate.astype(jnp.bfloat16)
    rows, cols = rounded.shape
    groups, steps = lax.axis_size("zh"), lax.axis_size("zl")
    slabs = groups * steps
    chips = lax.axis_size(PLANE)
    total_cols = cols * chips
    slab, core = lax.axis_index(LINE), lax.axis_index("core")
    residue = lax.axis_index("zl")
    own = lax.ppermute(rounded, ("ylo", "core"), TURN)
    other = lax.ppermute(own, "core", SWAP)
    both = jnp.concatenate([own, other], 0)
    near, far = [own], [other]
    for step in range(1, slabs // 2):
        near.append(onward(near[-1]))
        far.append(onward(far[-1]))
    near.append(onward(near[-1]))
    back = swap(far[1:4]) + swap(far[4:6]) + swap(far[6:])
    half = jnp.concatenate(near[::-1] + back, 0)
    gram = nt(half, both).reshape(slabs, chips, rows // chips, 2 * rows)
    gram = gram.transpose(1, 0, 2, 3).reshape(chips, rows, 2 * rows)
    gram, slab, core, residue = lax.optimization_barrier((gram, slab, core, residue))
    gram = lax.all_to_all(gram, PLANE, 0, 0)
    gram, half, own, slab, core, residue = lax.optimization_barrier(
        (gram, half, own, slab, core, residue)
    )
    gram = gram.sum(0).reshape(slabs, rows // chips, 2 * rows) / total_cols
    gram = jnp.where(core == 0, gram, gram[::-1])
    gram = turn_to(gram, slabs + slabs // 2 - core - slab)
    gram_low = gram.astype(jnp.bfloat16)
    gram, gram_low = gram.reshape(rows, 2 * rows), gram_low.reshape(rows, 2 * rows)
    panel = share(gram_low, chips).reshape(chips, slabs, rows // chips, 2 * rows)
    panel = panel.transpose(1, 0, 2, 3).reshape(groups, steps, rows, 2 * rows)
    here = lax.all_gather(gram_low, "zh", axis=0)
    panel, _ = lax.optimization_barrier((panel, here))
    cut = groups // 2
    left = (
        here,
        along(here, -1),
        along(here, 1),
        jnp.concatenate([along(here[:cut], -2), along(here[cut:], 2)], 0),
    )
    right_own = [
        lax.dynamic_index_in_dim(panel, (residue + shift) % steps, 1, False)
        for shift in (0, 1, steps - 1, 2)
    ]
    right_other = lax.ppermute(jnp.stack(right_own), "core", SWAP)
    right_other = jnp.concatenate(
        [right_other[:, :, :, rows:], right_other[:, :, :, :rows]], 3
    )
    square = 0.0
    for place in range(steps):
        square = square + mix(left[place][:, :, :rows], right_own[place])
    for place in range(steps):
        square = square + mix(left[place][:, :, rows:], right_other[place])
    poly = (-4.775 * gram + 2.0315 * square).astype(jnp.bfloat16)
    poly = poly.reshape(slabs, rows // chips, 2 * rows)
    poly = turn_to(poly, slabs // 2 + slab + core)
    poly = jnp.where(core == 0, poly, poly[::-1])
    panel = share(poly, chips).transpose(1, 0, 2, 3).reshape(slabs * rows, 2 * rows)
    away = tn(panel[:, rows:], half).astype(jnp.bfloat16)
    away = lax.ppermute(away, ("ylo", "core"), CROSS)
    stay = tn(panel[:, :rows], half) + 3.4445 * own.astype(jnp.float32)
    stay = lax.ppermute(stay.astype(jnp.bfloat16), ("ylo", "core"), TURN)
    return stay.astype(jnp.float32) + away.astype(jnp.float32)


def solution(mesh):
    fine = Mesh(mesh.devices.reshape(SIZES), AXES)
    spec = P(("zh", "zl", "ylo"), ("x", "yhi", "core"))
    return jax.shard_map(
        per_device, mesh=fine, in_specs=(spec,), out_specs=spec, check_vma=False
    )
```

```python
import jax
import jax.numpy as jnp
from jax import lax
from jax.sharding import Mesh, PartitionSpec as P

AXES = ("zh", "zl", "ylo", "x", "yhi", "core")
SIZES = (4, 4, 2, 4, 2, 2)
LINE = ("zh", "zl")
PLANE = ("ylo", "x", "yhi")
SWAP = ((0, 1), (1, 0))
TURN = ((0, 0), (1, 2), (2, 1), (3, 3))
CROSS = ((0, 2), (1, 0), (2, 3), (3, 1))


def share(piece, size):
    copies = jnp.broadcast_to(piece[None], (size,) + piece.shape)
    return lax.all_to_all(copies, PLANE, 0, 0)


def along(piece, shift):
    size = lax.axis_size(LINE)
    pairs = [(place, (place + shift) % size) for place in range(size)]
    return lax.ppermute(piece, LINE, pairs)


def onward(piece):
    size = lax.axis_size(LINE)
    pairs = [
        (2 * place + core, 2 * ((place + 1 - 2 * core) % size) + core)
        for place in range(size)
        for core in range(2)
    ]
    return lax.ppermute(piece, LINE + ("core",), pairs)


def swap(pieces):
    return list(lax.ppermute(jnp.stack(pieces), "core", SWAP))


def mix(left, right):
    return lax.dot_general(
        left, right, (((0, 2), (0, 1)), ((), ())), preferred_element_type=jnp.float32
    )


def nt(left, right):
    return lax.dot_general(
        left, right, (((1,), (1,)), ((), ())), preferred_element_type=jnp.float32
    )


def tn(left, right):
    return lax.dot_general(
        left, right, (((0,), (0,)), ((), ())), preferred_element_type=jnp.float32
    )


def wide(halves):
    return jnp.concatenate([halves[0], halves[1]], 1)


def turn_to(blocks, start):
    size = blocks.shape[1]
    return lax.dynamic_slice_in_dim(
        jnp.concatenate([blocks, blocks], 1), start % size, size, 1
    )


def per_device(iterate):
    rounded = iterate.astype(jnp.bfloat16)
    rows, cols = rounded.shape
    groups, steps = lax.axis_size("zh"), lax.axis_size("zl")
    slabs = groups * steps
    chips = lax.axis_size(PLANE)
    total_cols = cols * chips
    slab, core = lax.axis_index(LINE), lax.axis_index("core")
    residue = lax.axis_index("zl")
    own = lax.ppermute(rounded, ("ylo", "core"), TURN)
    other = lax.ppermute(own, "core", SWAP)
    near, far = [own], [other]
    for step in range(1, slabs // 2):
        near.append(onward(near[-1]))
        far.append(onward(far[-1]))
    near.append(onward(near[-1]))
    back = swap(far[1:4]) + swap(far[4:6]) + swap(far[6:])
    half = jnp.concatenate(near[::-1] + back, 0)
    gram = jnp.stack([nt(half, own), nt(half, other)])
    gram = gram.reshape(2, slabs, chips, rows // chips, rows)
    gram = gram.transpose(2, 0, 1, 3, 4).reshape(chips, 2 * rows, rows)
    gram, slab, core, residue = lax.optimization_barrier((gram, slab, core, residue))
    gram = lax.all_to_all(gram, PLANE, 0, 0)
    gram, half, own, slab, core, residue = lax.optimization_barrier(
        (gram, half, own, slab, core, residue)
    )
    gram = gram.sum(0).reshape(2, slabs, rows // chips, rows) / total_cols
    gram = jnp.where(core == 0, gram, gram[:, ::-1])
    gram = turn_to(gram, slabs + slabs // 2 - core - slab)
    gram_low = gram.astype(jnp.bfloat16).reshape(2 * rows, rows)
    gram = wide(gram.reshape(2, rows, rows))
    panel = share(gram_low, chips).reshape(chips, 2, slabs, rows // chips, rows)
    panel = panel.transpose(2, 0, 3, 1, 4).reshape(groups, steps, rows, 2 * rows)
    here = lax.all_gather(gram_low, "zh", axis=0).reshape(groups, 2, rows, rows)
    panel, _ = lax.optimization_barrier((panel, here))
    cut = groups // 2
    left = (
        here,
        along(here, -1),
        along(here, 1),
        jnp.concatenate([along(here[:cut], -2), along(here[cut:], 2)], 0),
    )
    right_own = [
        lax.dynamic_index_in_dim(panel, (residue + shift) % steps, 1, False)
        for shift in (0, 1, steps - 1, 2)
    ]
    right_other = lax.ppermute(jnp.stack(right_own), "core", SWAP)
    right_other = jnp.concatenate(
        [right_other[:, :, :, rows:], right_other[:, :, :, :rows]], 3
    )
    square = 0.0
    for place in range(steps):
        square = square + mix(left[place][:, 0], right_own[place])
    for place in range(steps):
        square = square + mix(left[place][:, 1], right_other[place])
    poly = (-4.775 * gram + 2.0315 * square).astype(jnp.bfloat16)
    poly = poly.reshape(slabs, rows // chips, 2, rows).transpose(2, 0, 1, 3)
    poly = turn_to(poly, slabs // 2 + slab + core)
    poly = jnp.where(core == 0, poly, poly[:, ::-1])
    panel = share(poly.reshape(2 * rows, rows), chips)
    panel = panel.reshape(chips, 2, slabs, rows // chips, rows)
    panel = panel.transpose(2, 0, 3, 1, 4).reshape(slabs * rows, 2 * rows)
    away = tn(panel[:, rows:], half).astype(jnp.bfloat16)
    away = lax.ppermute(away, ("ylo", "core"), CROSS)
    stay = tn(panel[:, :rows], half) + 3.4445 * own.astype(jnp.float32)
    stay = lax.ppermute(stay.astype(jnp.bfloat16), ("ylo", "core"), TURN)
    return stay.astype(jnp.float32) + away.astype(jnp.float32)


def solution(mesh):
    fine = Mesh(mesh.devices.reshape(SIZES), AXES)
    spec = P(("zh", "zl", "ylo"), ("x", "yhi", "core"))
    return jax.shard_map(
        per_device, mesh=fine, in_specs=(spec,), out_specs=spec, check_vma=False
    )
```

```python
import jax
import jax.numpy as jnp
from jax import lax
from jax.sharding import Mesh, PartitionSpec as P

AXES = ("zh", "zl", "ylo", "x", "yhi", "core")
SIZES = (4, 4, 2, 4, 2, 2)
LINE = ("zh", "zl")
PLANE = ("ylo", "x", "yhi")
SWAP = ((0, 1), (1, 0))
TURN = ((0, 0), (1, 2), (2, 1), (3, 3))
CROSS = ((0, 2), (1, 0), (2, 3), (3, 1))


def share(piece, size):
    copies = jnp.broadcast_to(piece[None], (size,) + piece.shape)
    return lax.all_to_all(copies, PLANE, 0, 0)


def along(piece, shift):
    size = lax.axis_size(LINE)
    pairs = [(place, (place + shift) % size) for place in range(size)]
    return lax.ppermute(piece, LINE, pairs)


def onward(piece):
    size = lax.axis_size(LINE)
    pairs = [
        (2 * place + core, 2 * ((place + 1 - 2 * core) % size) + core)
        for place in range(size)
        for core in range(2)
    ]
    return lax.ppermute(piece, LINE + ("core",), pairs)


def swap(pieces):
    return list(lax.ppermute(jnp.stack(pieces), "core", SWAP))


def mix(left, right):
    return lax.dot_general(
        left, right, (((0, 2), (0, 1)), ((), ())), preferred_element_type=jnp.float32
    )


def nt(left, right):
    return lax.dot_general(
        left, right, (((1,), (1,)), ((), ())), preferred_element_type=jnp.float32
    )


def tn(left, right):
    return lax.dot_general(
        left, right, (((0,), (0,)), ((), ())), preferred_element_type=jnp.float32
    )


def wide(halves):
    return jnp.concatenate([halves[0], halves[1]], 1)


def turn_to(blocks, start):
    size = blocks.shape[1]
    return lax.dynamic_slice_in_dim(
        jnp.concatenate([blocks, blocks], 1), start % size, size, 1
    )


def per_device(iterate):
    rounded = iterate.astype(jnp.bfloat16)
    rows, cols = rounded.shape
    groups, steps = lax.axis_size("zh"), lax.axis_size("zl")
    slabs = groups * steps
    chips = lax.axis_size(PLANE)
    total_cols = cols * chips
    slab, core = lax.axis_index(LINE), lax.axis_index("core")
    residue = lax.axis_index("zl")
    own = lax.ppermute(rounded, ("ylo", "core"), TURN)
    other = lax.ppermute(own, "core", SWAP)
    near, far = [own], [other]
    for step in range(1, slabs // 2):
        near.append(onward(near[-1]))
        far.append(onward(far[-1]))
    near.append(onward(near[-1]))
    back = swap(far[1:4]) + swap(far[4:6]) + swap(far[6:])
    half = jnp.concatenate(near[::-1] + back, 0)
    exact = [nt(half, side) for side in (own, other)]
    parts = [lax.reduce_precision(side, 8, 7) for side in exact]
    middle = slabs // 2
    begin, end = middle * rows, (middle + 1) * rows
    rest = [one[begin:end] - two[begin:end] for one, two in zip(exact, parts)]
    parts = [
        jnp.stack(sides).astype(jnp.bfloat16).reshape(2, -1, chips, rows // chips, rows)
        for sides in (parts, rest)
    ]
    parts = [
        part.transpose(2, 0, 1, 3, 4).reshape(chips, -1, rows) for part in parts
    ]
    parts = jnp.concatenate(parts, 1)
    parts, slab, core, residue = lax.optimization_barrier((parts, slab, core, residue))
    parts = lax.all_to_all(parts, PLANE, 0, 0)
    parts, half, own, slab, core, residue = lax.optimization_barrier(
        (parts, half, own, slab, core, residue)
    )
    gram = parts.astype(jnp.float32).sum(0) / total_cols
    rest = gram[2 * rows :].reshape(2, 1, rows // chips, rows)
    gram = gram[: 2 * rows].reshape(2, slabs, rows // chips, rows)
    gram = jnp.concatenate(
        [gram[:, :middle], gram[:, middle : middle + 1] + rest, gram[:, middle + 1 :]], 1
    )
    gram = jnp.where(core == 0, gram, gram[:, ::-1])
    gram = turn_to(gram, slabs + slabs // 2 - core - slab)
    gram_low = gram.astype(jnp.bfloat16).reshape(2 * rows, rows)
    gram = wide(gram.reshape(2, rows, rows))
    panel = share(gram_low, chips).reshape(chips, 2, slabs, rows // chips, rows)
    panel = panel.transpose(2, 0, 3, 1, 4).reshape(groups, steps, rows, 2 * rows)
    here = lax.all_gather(gram_low, "zh", axis=0).reshape(groups, 2, rows, rows)
    here = here.transpose(1, 0, 2, 3)
    panel, _ = lax.optimization_barrier((panel, here))
    left = (
        here,
        along(here, -1),
        along(here, 1),
        (along(here[0], -2), along(here[1], 2)),
    )
    right_own = [
        lax.dynamic_index_in_dim(panel, (residue + shift) % steps, 1, False)
        for shift in (0, 1, steps - 1, 2)
    ]
    right_other = lax.ppermute(jnp.stack(right_own), "core", SWAP)
    square = sum(mix(left[place][0], right_own[place]) for place in range(steps))
    across = sum(mix(left[place][1], right_other[place]) for place in range(steps))
    square = square + jnp.concatenate([across[:, rows:], across[:, :rows]], 1)
    poly = (-4.775 * gram + 2.0315 * square).astype(jnp.bfloat16)
    poly = poly.reshape(slabs, rows // chips, 2, rows).transpose(2, 0, 1, 3)
    poly = turn_to(poly, slabs // 2 + slab + core)
    poly = jnp.where(core == 0, poly, poly[:, ::-1])
    panel = share(poly.reshape(2 * rows, rows), chips)
    panel = panel.reshape(chips, 2, slabs, rows // chips, rows)
    panel = panel.transpose(2, 0, 3, 1, 4).reshape(slabs * rows, 2 * rows)
    away = tn(panel[:, rows:], half).astype(jnp.bfloat16)
    away = lax.ppermute(away, ("ylo", "core"), CROSS)
    stay = tn(panel[:, :rows], half) + 3.4445 * own.astype(jnp.float32)
    stay = lax.ppermute(stay.astype(jnp.bfloat16), ("ylo", "core"), TURN)
    return stay.astype(jnp.float32) + away.astype(jnp.float32)


def solution(mesh):
    fine = Mesh(mesh.devices.reshape(SIZES), AXES)
    spec = P(("zh", "zl", "ylo"), ("x", "yhi", "core"))
    return jax.shard_map(
        per_device, mesh=fine, in_specs=(spec,), out_specs=spec, check_vma=False
    )
```

```python
import jax
import jax.numpy as jnp
from jax import lax
from jax.sharding import Mesh, PartitionSpec as P

AXES = ("zh", "zl", "ylo", "x", "yhi", "core")
SIZES = (4, 4, 2, 4, 2, 2)
LINE = ("zh", "zl")
PLANE = ("ylo", "x", "yhi")
SWAP = ((0, 1), (1, 0))
TURN = ((0, 0), (1, 2), (2, 1), (3, 3))
CROSS = ((0, 2), (1, 0), (2, 3), (3, 1))


def share(piece, size):
    copies = jnp.broadcast_to(piece[None], (size,) + piece.shape)
    return lax.all_to_all(copies, PLANE, 0, 0)


def along(piece, shift, shift_of_core_1=None):
    size = lax.axis_size(LINE)
    shifts = (shift, shift if shift_of_core_1 is None else shift_of_core_1)
    pairs = [
        (2 * place + core, 2 * ((place + shifts[core]) % size) + core)
        for place in range(size)
        for core in range(2)
    ]
    return lax.ppermute(piece, LINE + ("core",), pairs)


def onward(piece):
    return along(piece, 1, -1)


def swap(pieces):
    return list(lax.ppermute(jnp.stack(pieces), "core", SWAP))


def mix(left, right):
    return lax.dot_general(
        left, right, (((0, 2), (0, 1)), ((), ())), preferred_element_type=jnp.float32
    )


def nt(left, right):
    return lax.dot_general(
        left, right, (((1,), (1,)), ((), ())), preferred_element_type=jnp.float32
    )


def tn(left, right):
    return lax.dot_general(
        left, right, (((0,), (0,)), ((), ())), preferred_element_type=jnp.float32
    )


def products(blocks, both, chips, whole=None):
    rows = both.shape[0] // 2
    exact = nt(blocks, both)
    parts = [lax.reduce_precision(exact, 8, 7)]
    if whole is not None:
        here = slice(whole * rows, (whole + 1) * rows)
        parts.append(exact[here] - parts[0][here])
    parts = [
        part.astype(jnp.bfloat16)
        .reshape(-1, chips, rows // chips, 2, rows)
        .transpose(1, 3, 0, 2, 4)
        .reshape(chips, -1, rows)
        for part in parts
    ]
    return jnp.concatenate(parts, 1)


def plane_sum(parts):
    return lax.all_to_all(parts, PLANE, 0, 0).astype(jnp.float32).sum(0)


def blocks_of(summed, count):
    rows = summed.shape[1]
    size = 2 * count * (rows // 16)
    blocks = summed[:size].reshape(2, count, -1, rows)
    if summed.shape[0] == size:
        return blocks
    rest = summed[size:].reshape(2, 1, -1, rows)
    return jnp.concatenate([blocks[:, :-1], blocks[:, -1:] + rest], 1)


def wide(halves):
    return jnp.concatenate([halves[0], halves[1]], 1)


def turn_to(blocks, start):
    size = blocks.shape[1]
    return lax.dynamic_slice_in_dim(
        jnp.concatenate([blocks, blocks], 1), start % size, size, 1
    )


def per_device(iterate):
    rounded = iterate.astype(jnp.bfloat16)
    rows, cols = rounded.shape
    groups, steps = lax.axis_size("zh"), lax.axis_size("zl")
    slabs = groups * steps
    chips = lax.axis_size(PLANE)
    total_cols = cols * chips
    slab, core = lax.axis_index(LINE), lax.axis_index("core")
    residue = lax.axis_index("zl")
    own = lax.ppermute(rounded, ("ylo", "core"), TURN)
    other = lax.ppermute(own, "core", SWAP)
    both = jnp.concatenate([own, other], 0)
    near, far = [own], [other]
    for step in range(1, slabs // 2):
        near.append(onward(near[-1]))
        far.append(onward(far[-1]))
    first = 6
    half_early = jnp.concatenate(near[first - 1 :: -1], 0)
    early = plane_sum(products(half_early, both, chips, first - 1))
    early, near[-1] = lax.optimization_barrier((early, near[-1]))
    near.append(onward(near[-1]))
    back = swap(far[1:4]) + swap(far[4:6]) + swap(far[6:])
    half_late = jnp.concatenate(near[: first - 1 : -1] + back, 0)
    late = products(half_late, both, chips)
    early = blocks_of(early, first)
    late, early, slab, core, residue = lax.optimization_barrier(
        (late, early, slab, core, residue)
    )
    late = lax.all_to_all(late, PLANE, 0, 0)
    late, early, half_early, half_late, own, slab, core, residue = (
        lax.optimization_barrier(
            (late, early, half_early, half_late, own, slab, core, residue)
        )
    )
    late = blocks_of(late.astype(jnp.float32).sum(0), slabs - first)
    ahead = slabs // 2 + 1 - first
    gram = jnp.concatenate([late[:, :ahead], early, late[:, ahead:]], 1) / total_cols
    gram = jnp.where(core == 0, gram, gram[:, ::-1])
    gram = turn_to(gram, slabs + slabs // 2 - core - slab)
    gram_low = gram.astype(jnp.bfloat16).reshape(2 * rows, rows)
    gram = wide(gram.reshape(2, rows, rows))
    panel = share(gram_low, chips).reshape(chips, 2, slabs, rows // chips, rows)
    panel = panel.transpose(2, 0, 3, 1, 4).reshape(groups, steps, rows, 2 * rows)
    here = lax.all_gather(gram_low, "zh", axis=0).reshape(groups, 2, rows, rows)
    here = here.transpose(1, 0, 2, 3)
    panel, _ = lax.optimization_barrier((panel, here))
    left = (
        here,
        along(here, -1),
        along(here, 1),
        along(here, -2, 2),
    )
    right_own = [
        lax.dynamic_index_in_dim(panel, (residue + shift) % steps, 1, False)
        for shift in (0, 1, steps - 1, 2)
    ]
    right_other = lax.ppermute(jnp.stack(right_own), "core", SWAP)
    square = sum(mix(left[place][0], right_own[place]) for place in range(steps))
    across = sum(mix(left[place][1], right_other[place]) for place in range(steps))
    square = square + jnp.concatenate([across[:, rows:], across[:, :rows]], 1)
    poly = (-4.775 * gram + 2.0315 * square).astype(jnp.bfloat16)
    poly = poly.reshape(slabs, rows // chips, 2, rows).transpose(2, 0, 1, 3)
    poly = turn_to(poly, slabs // 2 + slab + core)
    poly = jnp.where(core == 0, poly, poly[:, ::-1])
    panel = share(poly.reshape(2 * rows, rows), chips)
    panel = panel.reshape(chips, 2, slabs, rows // chips, rows)
    panel = panel.transpose(2, 0, 3, 1, 4).reshape(slabs * rows, 2 * rows)
    panel = panel.reshape(slabs, rows, 2 * rows)
    panel_early = panel[ahead : ahead + first].reshape(first * rows, 2 * rows)
    panel_late = jnp.concatenate([panel[:ahead], panel[ahead + first :]], 0)
    panel_late = panel_late.reshape((slabs - first) * rows, 2 * rows)
    away, stay = (
        tn(panel_early[:, part], half_early) + tn(panel_late[:, part], half_late)
        for part in (slice(rows, None), slice(rows))
    )
    away = lax.ppermute(away.astype(jnp.bfloat16), ("ylo", "core"), CROSS)
    stay = stay + 3.4445 * own.astype(jnp.float32)
    stay = lax.ppermute(stay.astype(jnp.bfloat16), ("ylo", "core"), TURN)
    return stay.astype(jnp.float32) + away.astype(jnp.float32)


def solution(mesh):
    fine = Mesh(mesh.devices.reshape(SIZES), AXES)
    spec = P(("zh", "zl", "ylo"), ("x", "yhi", "core"))
    return jax.shard_map(
        per_device, mesh=fine, in_specs=(spec,), out_specs=spec, check_vma=False
    )
```

```python
import jax
import jax.numpy as jnp
from jax import lax
from jax.sharding import Mesh, PartitionSpec as P

AXES = ("zh", "zl", "ylo", "x", "yhi", "core")
SIZES = (4, 4, 2, 4, 2, 2)
LINE = ("zh", "zl")
PLANE = ("ylo", "x", "yhi")
SWAP = ((0, 1), (1, 0))
TURN = ((0, 0), (1, 2), (2, 1), (3, 3))
CROSS = ((0, 2), (1, 0), (2, 3), (3, 1))


def share(piece, size):
    copies = jnp.broadcast_to(piece[None], (size,) + piece.shape)
    return lax.all_to_all(copies, PLANE, 0, 0)


def along(piece, shift, shift_of_core_1=None):
    size = lax.axis_size(LINE)
    shifts = (shift, shift if shift_of_core_1 is None else shift_of_core_1)
    pairs = [
        (2 * place + core, 2 * ((place + shifts[core]) % size) + core)
        for place in range(size)
        for core in range(2)
    ]
    return lax.ppermute(piece, LINE + ("core",), pairs)


def split(value):
    terms = []
    for _ in range(3):
        terms.append(lax.reduce_precision(value, 8, 7))
        value = value - terms[-1]
    return jnp.stack(terms)


def mix(left, right):
    return lax.dot_general(
        left, right, (((0, 2), (0, 1)), ((), ())), preferred_element_type=jnp.float32
    )


def per_device(iterate):
    rounded = iterate.astype(jnp.bfloat16)
    rows, cols = rounded.shape
    groups, steps = lax.axis_size("zh"), lax.axis_size("zl")
    chips = lax.axis_size(PLANE)
    total_cols = cols * chips
    own = lax.ppermute(rounded, ("ylo", "core"), TURN)
    half = lax.all_gather(own, LINE, axis=0)
    other = lax.ppermute(own, "core", SWAP)
    partial_gram = lax.dot_general(
        jnp.concatenate([own, other], 0),
        half,
        (((1,), (2,)), ((), ())),
        preferred_element_type=jnp.float32,
    )
    partial_gram = partial_gram.transpose(1, 0, 2).astype(jnp.bfloat16)
    wide = own.astype(jnp.float32)
    extra = jnp.pad(split((wide * wide).sum(1)), ((0, 13), (0, 0)))
    extra = jnp.broadcast_to(extra.astype(jnp.bfloat16)[None], (chips, 16, rows))
    partial_gram = jnp.concatenate([partial_gram, extra], 1)
    met = lax.axis_index(PLANE) == lax.axis_index(LINE)
    residue = lax.axis_index("zl")
    partial_gram, met, residue = lax.optimization_barrier((partial_gram, met, residue))
    summands = lax.all_to_all(partial_gram, PLANE, 0, 0)
    summands, own, half, met, residue = lax.optimization_barrier(
        (summands, own, half, met, residue)
    )
    gram = summands.astype(jnp.float32).sum(0) / total_cols
    diagonal = gram[2 * rows :].sum(0)
    gram = gram[: 2 * rows]
    place = lax.broadcasted_iota(jnp.int32, gram.shape, 0)
    place = place - lax.broadcasted_iota(jnp.int32, gram.shape, 1)
    gram = jnp.where((place == 0) & met, diagonal[None], gram)
    gram_low = gram.astype(jnp.bfloat16)
    panel = share(gram_low, chips).reshape(groups, steps, 2 * rows, rows)
    here = lax.all_gather(gram_low, "zh", axis=0)
    panel, _ = lax.optimization_barrier((panel, here))
    right = (
        here,
        along(here, -1),
        along(here, 1),
        along(here, -2, 2),
    )
    left_own = [
        lax.dynamic_index_in_dim(panel, (residue + shift) % steps, 1, False)
        for shift in (0, 1, steps - 1, 2)
    ]
    left_other = lax.ppermute(jnp.stack(left_own), "core", SWAP)
    left_other = jnp.concatenate(
        [left_other[:, :, rows:], left_other[:, :, :rows]], 2
    )
    square = 0.0
    for place in range(steps):
        square = square + mix(left_own[place], right[place][:, :rows])
    for place in range(steps):
        square = square + mix(left_other[place], right[place][:, rows:])
    poly = (-4.775 * gram + 2.0315 * square).astype(jnp.bfloat16)
    panel = share(poly, chips)
    away = mix(panel[:, rows:], half).astype(jnp.bfloat16)
    away = lax.ppermute(away, ("ylo", "core"), CROSS)
    stay = mix(panel[:, :rows], half) + 3.4445 * own.astype(jnp.float32)
    stay = lax.ppermute(stay.astype(jnp.bfloat16), ("ylo", "core"), TURN)
    return stay.astype(jnp.float32) + away.astype(jnp.float32)


def solution(mesh):
    fine = Mesh(mesh.devices.reshape(SIZES), AXES)
    spec = P(("zh", "zl", "ylo"), ("x", "yhi", "core"))
    return jax.shard_map(
        per_device, mesh=fine, in_specs=(spec,), out_specs=spec, check_vma=False
    )
```

```python
import jax
import jax.numpy as jnp
from jax import lax
from jax.sharding import Mesh, PartitionSpec as P

AXES = ("zh", "zl", "ylo", "x", "yhi", "core")
SIZES = (4, 4, 2, 4, 2, 2)
LINE = ("zh", "zl")
PLANE = ("ylo", "x", "yhi")
SWAP = ((0, 1), (1, 0))
TURN = ((0, 0), (1, 2), (2, 1), (3, 3))
CROSS = ((0, 2), (1, 0), (2, 3), (3, 1))


def share(piece, size):
    copies = jnp.broadcast_to(piece[None], (size,) + piece.shape)
    return lax.all_to_all(copies, PLANE, 0, 0)


def along(piece, shift, shift_of_core_1=None):
    size = lax.axis_size(LINE)
    shifts = (shift, shift if shift_of_core_1 is None else shift_of_core_1)
    pairs = [
        (2 * place + core, 2 * ((place + shifts[core]) % size) + core)
        for place in range(size)
        for core in range(2)
    ]
    return lax.ppermute(piece, LINE + ("core",), pairs)


def onward(piece):
    return along(piece, 1, -1)


def swap(pieces):
    return list(lax.ppermute(jnp.stack(pieces), "core", SWAP))


def put(blocks, block, place):
    return lax.dynamic_update_index_in_dim(blocks, block, place, 0)


def split(value):
    terms = []
    for _ in range(3):
        terms.append(lax.reduce_precision(value, 8, 7))
        value = value - terms[-1]
    return jnp.stack(terms)


def mix(left, right):
    return lax.dot_general(
        left, right, (((0, 2), (0, 1)), ((), ())), preferred_element_type=jnp.float32
    )


def per_device(iterate):
    rounded = iterate.astype(jnp.bfloat16)
    rows, cols = rounded.shape
    groups, steps = lax.axis_size("zh"), lax.axis_size("zl")
    chips = lax.axis_size(PLANE)
    total_cols = cols * chips
    own = lax.ppermute(rounded, ("ylo", "core"), TURN)
    other = lax.ppermute(own, "core", SWAP)
    slabs = groups * steps
    near, far = [own], [other]
    for step in range(1, slabs // 2):
        near.append(onward(near[-1]))
        far.append(onward(far[-1]))
    near.append(onward(near[-1]))
    back = [None] + swap(far[1:4]) + swap(far[4:6]) + swap(far[6:])
    slab, toward = lax.axis_index(LINE), 1 - 2 * lax.axis_index("core")
    half = jnp.zeros((slabs, rows, cols), jnp.bfloat16)
    for step in range(slabs // 2 + 1):
        half = put(half, near[step], (slab - step * toward) % slabs)
        if 0 < step < slabs // 2:
            half = put(half, back[step], (slab + step * toward) % slabs)
    partial_gram = lax.dot_general(
        jnp.concatenate([own, other], 0),
        half,
        (((1,), (2,)), ((), ())),
        preferred_element_type=jnp.float32,
    )
    partial_gram = partial_gram.transpose(1, 0, 2).astype(jnp.bfloat16)
    wide = own.astype(jnp.float32)
    extra = jnp.pad(split((wide * wide).sum(1)), ((0, 13), (0, 0)))
    extra = jnp.broadcast_to(extra.astype(jnp.bfloat16)[None], (chips, 16, rows))
    partial_gram = jnp.concatenate([partial_gram, extra], 1)
    met = lax.axis_index(PLANE) == lax.axis_index(LINE)
    residue = lax.axis_index("zl")
    partial_gram, met, residue = lax.optimization_barrier((partial_gram, met, residue))
    summands = lax.all_to_all(partial_gram, PLANE, 0, 0)
    summands, own, half, met, residue = lax.optimization_barrier(
        (summands, own, half, met, residue)
    )
    gram = summands.astype(jnp.float32).sum(0) / total_cols
    diagonal = gram[2 * rows :].sum(0)
    gram = gram[: 2 * rows]
    place = lax.broadcasted_iota(jnp.int32, gram.shape, 0)
    place = place - lax.broadcasted_iota(jnp.int32, gram.shape, 1)
    gram = jnp.where((place == 0) & met, diagonal[None], gram)
    gram_low = gram.astype(jnp.bfloat16)
    panel = share(gram_low, chips).reshape(groups, steps, 2 * rows, rows)
    here = lax.all_gather(gram_low, "zh", axis=0)
    panel, _ = lax.optimization_barrier((panel, here))
    right = (
        here,
        along(here, -1),
        along(here, 1),
        along(here, -2, 2),
    )
    left_own = [
        lax.dynamic_index_in_dim(panel, (residue + shift) % steps, 1, False)
        for shift in (0, 1, steps - 1, 2)
    ]
    left_other = lax.ppermute(jnp.stack(left_own), "core", SWAP)
    left_other = jnp.concatenate(
        [left_other[:, :, rows:], left_other[:, :, :rows]], 2
    )
    square = 0.0
    for place in range(steps):
        square = square + mix(left_own[place], right[place][:, :rows])
    for place in range(steps):
        square = square + mix(left_other[place], right[place][:, rows:])
    poly = (-4.775 * gram + 2.0315 * square).astype(jnp.bfloat16)
    panel = share(poly, chips)
    away = mix(panel[:, rows:], half).astype(jnp.bfloat16)
    away = lax.ppermute(away, ("ylo", "core"), CROSS)
    stay = mix(panel[:, :rows], half) + 3.4445 * own.astype(jnp.float32)
    stay = lax.ppermute(stay.astype(jnp.bfloat16), ("ylo", "core"), TURN)
    return stay.astype(jnp.float32) + away.astype(jnp.float32)


def solution(mesh):
    fine = Mesh(mesh.devices.reshape(SIZES), AXES)
    spec = P(("zh", "zl", "ylo"), ("x", "yhi", "core"))
    return jax.shard_map(
        per_device, mesh=fine, in_specs=(spec,), out_specs=spec, check_vma=False
    )
```

```python
import jax
import jax.numpy as jnp
from jax import lax
from jax.sharding import Mesh, PartitionSpec as P

AXES = ("zh", "zl", "ylo", "x", "yhi", "core")
SIZES = (4, 4, 2, 4, 2, 2)
LINE = ("zh", "zl")
PLANE = ("ylo", "x", "yhi")
SWAP = ((0, 1), (1, 0))
TURN = ((0, 0), (1, 2), (2, 1), (3, 3))
CROSS = ((0, 2), (1, 0), (2, 3), (3, 1))


def share(piece, size):
    copies = jnp.broadcast_to(piece[None], (size,) + piece.shape)
    return lax.all_to_all(copies, PLANE, 0, 0)


def along(piece, shift, shift_of_core_1=None):
    size = lax.axis_size(LINE)
    shifts = (shift, shift if shift_of_core_1 is None else shift_of_core_1)
    pairs = [
        (2 * place + core, 2 * ((place + shifts[core]) % size) + core)
        for place in range(size)
        for core in range(2)
    ]
    return lax.ppermute(piece, LINE + ("core",), pairs)


def onward(piece):
    return along(piece, 1, -1)


def launch(piece, side):
    size = lax.axis_size(LINE)
    pairs = []
    for place in range(size):
        for ylo in range(2):
            for core in range(2):
                to = ylo ^ side
                ahead = (place + 1 - 2 * to) % size
                pairs.append(
                    (4 * place + 2 * ylo + core, 4 * ahead + 2 * core + to)
                )
    return lax.ppermute(piece, LINE + ("ylo", "core"), pairs)


def swap(pieces):
    return list(lax.ppermute(jnp.stack(pieces), "core", SWAP))


def put(blocks, block, place):
    return lax.dynamic_update_index_in_dim(blocks, block, place, 0)


def split(value):
    terms = []
    for _ in range(3):
        terms.append(lax.reduce_precision(value, 8, 7))
        value = value - terms[-1]
    return jnp.stack(terms)


def mix(left, right):
    return lax.dot_general(
        left, right, (((0, 2), (0, 1)), ((), ())), preferred_element_type=jnp.float32
    )


def per_device(iterate):
    rounded = iterate.astype(jnp.bfloat16)
    rows, cols = rounded.shape
    groups, steps = lax.axis_size("zh"), lax.axis_size("zl")
    chips = lax.axis_size(PLANE)
    total_cols = cols * chips
    own = lax.ppermute(rounded, ("ylo", "core"), TURN)
    other = lax.ppermute(own, "core", SWAP)
    slabs = groups * steps
    near, far = [own, launch(rounded, 0)], [None, launch(rounded, 1)]
    for step in range(2, slabs // 2):
        near.append(onward(near[-1]))
        far.append(onward(far[-1]))
    near.append(onward(near[-1]))
    back = [None] + swap(far[1:4]) + swap(far[4:6]) + swap(far[6:])
    slab, toward = lax.axis_index(LINE), 1 - 2 * lax.axis_index("core")
    half = jnp.zeros((slabs, rows, cols), jnp.bfloat16)
    for step in range(slabs // 2 + 1):
        half = put(half, near[step], (slab - step * toward) % slabs)
        if 0 < step < slabs // 2:
            half = put(half, back[step], (slab + step * toward) % slabs)
    partial_gram = lax.dot_general(
        jnp.concatenate([own, other], 0),
        half,
        (((1,), (2,)), ((), ())),
        preferred_element_type=jnp.float32,
    )
    partial_gram = partial_gram.transpose(1, 0, 2).astype(jnp.bfloat16)
    wide = own.astype(jnp.float32)
    extra = jnp.pad(split((wide * wide).sum(1)), ((0, 13), (0, 0)))
    extra = jnp.broadcast_to(extra.astype(jnp.bfloat16)[None], (chips, 16, rows))
    partial_gram = jnp.concatenate([partial_gram, extra], 1)
    met = lax.axis_index(PLANE) == lax.axis_index(LINE)
    residue = lax.axis_index("zl")
    partial_gram, met, residue = lax.optimization_barrier((partial_gram, met, residue))
    summands = lax.all_to_all(partial_gram, PLANE, 0, 0)
    summands, own, half, met, residue = lax.optimization_barrier(
        (summands, own, half, met, residue)
    )
    gram = summands.astype(jnp.float32).sum(0) / total_cols
    diagonal = gram[2 * rows :].sum(0)
    gram = gram[: 2 * rows]
    place = lax.broadcasted_iota(jnp.int32, gram.shape, 0)
    place = place - lax.broadcasted_iota(jnp.int32, gram.shape, 1)
    gram = jnp.where((place == 0) & met, diagonal[None], gram)
    gram_low = gram.astype(jnp.bfloat16)
    panel = share(gram_low, chips).reshape(groups, steps, 2 * rows, rows)
    here = lax.all_gather(gram_low, "zh", axis=0)
    panel, _ = lax.optimization_barrier((panel, here))
    right = (
        here,
        along(here, -1),
        along(here, 1),
        along(here, -2, 2),
    )
    left_own = [
        lax.dynamic_index_in_dim(panel, (residue + shift) % steps, 1, False)
        for shift in (0, 1, steps - 1, 2)
    ]
    left_other = lax.ppermute(jnp.stack(left_own), "core", SWAP)
    left_other = jnp.concatenate(
        [left_other[:, :, rows:], left_other[:, :, :rows]], 2
    )
    square = 0.0
    for place in range(steps):
        square = square + mix(left_own[place], right[place][:, :rows])
    for place in range(steps):
        square = square + mix(left_other[place], right[place][:, rows:])
    poly = (-4.775 * gram + 2.0315 * square).astype(jnp.bfloat16)
    panel = share(poly, chips)
    away = mix(panel[:, rows:], half).astype(jnp.bfloat16)
    away = lax.ppermute(away, ("ylo", "core"), CROSS)
    stay = mix(panel[:, :rows], half) + 3.4445 * own.astype(jnp.float32)
    stay = lax.ppermute(stay.astype(jnp.bfloat16), ("ylo", "core"), TURN)
    return stay.astype(jnp.float32) + away.astype(jnp.float32)


def solution(mesh):
    fine = Mesh(mesh.devices.reshape(SIZES), AXES)
    spec = P(("zh", "zl", "ylo"), ("x", "yhi", "core"))
    return jax.shard_map(
        per_device, mesh=fine, in_specs=(spec,), out_specs=spec, check_vma=False
    )
```

```python
import jax
import jax.numpy as jnp
from jax import lax
from jax.sharding import Mesh, PartitionSpec as P

AXES = ("zh", "zl", "ylo", "x", "yhi", "core")
SIZES = (4, 4, 2, 4, 2, 2)
LINE = ("zh", "zl")
PLANE = ("ylo", "x", "yhi")
SWAP = ((0, 1), (1, 0))
TURN = ((0, 0), (1, 2), (2, 1), (3, 3))
CROSS = ((0, 2), (1, 0), (2, 3), (3, 1))


def share(piece, size):
    copies = jnp.broadcast_to(piece[None], (size,) + piece.shape)
    return lax.all_to_all(copies, PLANE, 0, 0)


def along(piece, shift, shift_of_core_1=None):
    size = lax.axis_size(LINE)
    shifts = (shift, shift if shift_of_core_1 is None else shift_of_core_1)
    pairs = [
        (2 * place + core, 2 * ((place + shifts[core]) % size) + core)
        for place in range(size)
        for core in range(2)
    ]
    return lax.ppermute(piece, LINE + ("core",), pairs)


def onward(piece):
    return along(piece, 1, -1)


def launch(piece, side):
    size = lax.axis_size(LINE)
    pairs = []
    for place in range(size):
        for ylo in range(2):
            for core in range(2):
                to = ylo ^ side
                ahead = (place + 1 - 2 * to) % size
                pairs.append(
                    (
                        4 * place + 2 * ylo + core,
                        4 * ahead + 2 * (core ^ side) + to,
                    )
                )
    return lax.ppermute(piece, LINE + ("ylo", "core"), pairs)


def swap(pieces):
    return list(lax.ppermute(jnp.stack(pieces), "core", SWAP))


def put(blocks, block, place):
    return lax.dynamic_update_index_in_dim(blocks, block, place, 0)


def split(value):
    terms = []
    for _ in range(3):
        terms.append(lax.reduce_precision(value, 8, 7))
        value = value - terms[-1]
    return jnp.stack(terms)


def mix(left, right):
    return lax.dot_general(
        left, right, (((0, 2), (0, 1)), ((), ())), preferred_element_type=jnp.float32
    )


def per_device(iterate):
    rounded = iterate.astype(jnp.bfloat16)
    rows, cols = rounded.shape
    groups, steps = lax.axis_size("zh"), lax.axis_size("zl")
    chips = lax.axis_size(PLANE)
    total_cols = cols * chips
    own = lax.ppermute(rounded, ("ylo", "core"), TURN)
    other = lax.ppermute(own, "core", SWAP)
    slabs = groups * steps
    near, far = [own, launch(rounded, 0)], [None, launch(swap([rounded])[0], 1)]
    for step in range(2, slabs // 2):
        near.append(onward(near[-1]))
        far.append(onward(far[-1]))
    near.append(onward(near[-1]))
    back = [None] + swap(far[1:4]) + swap(far[4:6]) + swap(far[6:])
    slab, toward = lax.axis_index(LINE), 1 - 2 * lax.axis_index("core")
    half = jnp.zeros((slabs, rows, cols), jnp.bfloat16)
    for step in range(slabs // 2 + 1):
        half = put(half, near[step], (slab - step * toward) % slabs)
        if 0 < step < slabs // 2:
            half = put(half, back[step], (slab + step * toward) % slabs)
    partial_gram = lax.dot_general(
        jnp.concatenate([own, other], 0),
        half,
        (((1,), (2,)), ((), ())),
        preferred_element_type=jnp.float32,
    )
    partial_gram = partial_gram.transpose(1, 0, 2).astype(jnp.bfloat16)
    wide = own.astype(jnp.float32)
    extra = jnp.pad(split((wide * wide).sum(1)), ((0, 13), (0, 0)))
    extra = jnp.broadcast_to(extra.astype(jnp.bfloat16)[None], (chips, 16, rows))
    partial_gram = jnp.concatenate([partial_gram, extra], 1)
    met = lax.axis_index(PLANE) == lax.axis_index(LINE)
    residue = lax.axis_index("zl")
    partial_gram, met, residue = lax.optimization_barrier((partial_gram, met, residue))
    summands = lax.all_to_all(partial_gram, PLANE, 0, 0)
    summands, own, half, met, residue = lax.optimization_barrier(
        (summands, own, half, met, residue)
    )
    gram = summands.astype(jnp.float32).sum(0) / total_cols
    diagonal = gram[2 * rows :].sum(0)
    gram = gram[: 2 * rows]
    place = lax.broadcasted_iota(jnp.int32, gram.shape, 0)
    place = place - lax.broadcasted_iota(jnp.int32, gram.shape, 1)
    gram = jnp.where((place == 0) & met, diagonal[None], gram)
    gram_low = gram.astype(jnp.bfloat16)
    panel = share(gram_low, chips).reshape(groups, steps, 2 * rows, rows)
    here = lax.all_gather(gram_low, "zh", axis=0)
    panel, _ = lax.optimization_barrier((panel, here))
    right = (
        here,
        along(here, -1),
        along(here, 1),
        along(here, -2, 2),
    )
    left_own = [
        lax.dynamic_index_in_dim(panel, (residue + shift) % steps, 1, False)
        for shift in (0, 1, steps - 1, 2)
    ]
    left_other = lax.ppermute(jnp.stack(left_own), "core", SWAP)
    left_other = jnp.concatenate(
        [left_other[:, :, rows:], left_other[:, :, :rows]], 2
    )
    square = 0.0
    for place in range(steps):
        square = square + mix(left_own[place], right[place][:, :rows])
    for place in range(steps):
        square = square + mix(left_other[place], right[place][:, rows:])
    poly = (-4.775 * gram + 2.0315 * square).astype(jnp.bfloat16)
    panel = share(poly, chips)
    away = mix(panel[:, rows:], half).astype(jnp.bfloat16)
    away = lax.ppermute(away, ("ylo", "core"), CROSS)
    stay = mix(panel[:, :rows], half) + 3.4445 * own.astype(jnp.float32)
    stay = lax.ppermute(stay.astype(jnp.bfloat16), ("ylo", "core"), TURN)
    return stay.astype(jnp.float32) + away.astype(jnp.float32)


def solution(mesh):
    fine = Mesh(mesh.devices.reshape(SIZES), AXES)
    spec = P(("zh", "zl", "ylo"), ("x", "yhi", "core"))
    return jax.shard_map(
        per_device, mesh=fine, in_specs=(spec,), out_specs=spec, check_vma=False
    )
```

```python
import jax
import jax.numpy as jnp
from jax import lax
from jax.sharding import Mesh, PartitionSpec as P

AXES = ("zh", "zl", "ylo", "x", "yhi", "core")
SIZES = (4, 4, 2, 4, 2, 2)
LINE = ("zh", "zl")
PLANE = ("ylo", "x", "yhi")
SWAP = ((0, 1), (1, 0))
TURN = ((0, 0), (1, 2), (2, 1), (3, 3))
CROSS = ((0, 2), (1, 0), (2, 3), (3, 1))


def share(piece, size):
    copies = jnp.broadcast_to(piece[None], (size,) + piece.shape)
    return lax.all_to_all(copies, PLANE, 0, 0)


def along(piece, shift, shift_of_core_1=None, cores=(0, 1)):
    size = lax.axis_size(LINE)
    shifts = (shift, shift if shift_of_core_1 is None else shift_of_core_1)
    pairs = [
        (2 * place + core, 2 * ((place + shifts[core]) % size) + core)
        for place in range(size)
        for core in cores
    ]
    return lax.ppermute(piece, LINE + ("core",), pairs)


def onward(piece, cores=(0, 1)):
    return along(piece, 1, -1, cores)


def launch(piece, side):
    size = lax.axis_size(LINE)
    pairs = []
    for place in range(size):
        for ylo in range(2):
            for core in range(2):
                to = ylo ^ side
                ahead = (place + 1 - 2 * to) % size
                pairs.append(
                    (
                        4 * place + 2 * ylo + core,
                        4 * ahead + 2 * (core ^ side) + to,
                    )
                )
    return lax.ppermute(piece, LINE + ("ylo", "core"), pairs)


def swap(pieces):
    return list(lax.ppermute(jnp.stack(pieces), "core", SWAP))


def put(blocks, block, place):
    return lax.dynamic_update_index_in_dim(blocks, block, place, 0)


def split(value):
    terms = []
    for _ in range(3):
        terms.append(lax.reduce_precision(value, 8, 7))
        value = value - terms[-1]
    return jnp.stack(terms)


def mix(left, right):
    return lax.dot_general(
        left, right, (((0, 2), (0, 1)), ((), ())), preferred_element_type=jnp.float32
    )


def per_device(iterate):
    rounded = iterate.astype(jnp.bfloat16)
    rows, cols = rounded.shape
    groups, steps = lax.axis_size("zh"), lax.axis_size("zl")
    chips = lax.axis_size(PLANE)
    total_cols = cols * chips
    own = lax.ppermute(rounded, ("ylo", "core"), TURN)
    other = lax.ppermute(own, "core", SWAP)
    slabs = groups * steps
    near, far = [own, launch(rounded, 0)], [None, launch(swap([rounded])[0], 1)]
    for step in range(2, slabs // 2):
        near.append(onward(near[-1]))
        far.append(onward(far[-1]))
    near_last, far_last = onward(near[-1], (1,)), onward(far[-1], (1,))
    back = [None] + swap(far[1:4]) + swap(far[4:6]) + swap(far[6:] + [far_last])
    slab, core = lax.axis_index(LINE), lax.axis_index("core")
    half = jnp.zeros((slabs, rows, cols), jnp.bfloat16)
    half = put(half, own, slab)
    for step in range(1, slabs // 2):
        ahead = step * (1 - 2 * core)
        half = put(half, near[step], (slab - ahead) % slabs)
        half = put(half, back[step], (slab + ahead) % slabs)
    last = jnp.where(core == 0, back[-1], near_last)
    half = put(half, last, (slab + slabs // 2) % slabs)
    partial_gram = lax.dot_general(
        jnp.concatenate([own, other], 0),
        half,
        (((1,), (2,)), ((), ())),
        preferred_element_type=jnp.float32,
    )
    partial_gram = partial_gram.transpose(1, 0, 2).astype(jnp.bfloat16)
    wide = own.astype(jnp.float32)
    extra = jnp.pad(split((wide * wide).sum(1)), ((0, 5), (0, 0)))
    extra = jnp.broadcast_to(extra.astype(jnp.bfloat16)[None], (chips, 8, rows))
    partial_gram = jnp.concatenate([partial_gram, extra], 1)
    met = lax.axis_index(PLANE) == lax.axis_index(LINE)
    residue = lax.axis_index("zl")
    partial_gram, met, residue = lax.optimization_barrier((partial_gram, met, residue))
    summands = lax.all_to_all(partial_gram, PLANE, 0, 0)
    summands, own, half, met, residue = lax.optimization_barrier(
        (summands, own, half, met, residue)
    )
    gram = summands.astype(jnp.float32).sum(0) / total_cols
    diagonal = gram[2 * rows :].sum(0)
    gram = gram[: 2 * rows]
    place = lax.broadcasted_iota(jnp.int32, gram.shape, 0)
    place = place - lax.broadcasted_iota(jnp.int32, gram.shape, 1)
    gram = jnp.where((place == 0) & met, diagonal[None], gram)
    gram_low = gram.astype(jnp.bfloat16)
    panel = share(gram_low, chips).reshape(groups, steps, 2 * rows, rows)
    here = lax.all_gather(gram_low, "zh", axis=0)
    panel, _ = lax.optimization_barrier((panel, here))
    right = (
        here,
        along(here, -1),
        along(here, 1),
        along(here, -2, 2),
    )
    left_own = [
        lax.dynamic_index_in_dim(panel, (residue + shift) % steps, 1, False)
        for shift in (0, 1, steps - 1, 2)
    ]
    left_other = lax.ppermute(jnp.stack(left_own), "core", SWAP)
    left_other = jnp.concatenate(
        [left_other[:, :, rows:], left_other[:, :, :rows]], 2
    )
    square = 0.0
    for place in range(steps):
        square = square + mix(left_own[place], right[place][:, :rows])
    for place in range(steps):
        square = square + mix(left_other[place], right[place][:, rows:])
    poly = (-4.775 * gram + 2.0315 * square).astype(jnp.bfloat16)
    panel = share(poly, chips)
    away = mix(panel[:, rows:], half).astype(jnp.bfloat16)
    away = lax.ppermute(away, ("ylo", "core"), CROSS)
    stay = mix(panel[:, :rows], half) + 3.4445 * own.astype(jnp.float32)
    stay = lax.ppermute(stay.astype(jnp.bfloat16), ("ylo", "core"), TURN)
    return stay.astype(jnp.float32) + away.astype(jnp.float32)


def solution(mesh):
    fine = Mesh(mesh.devices.reshape(SIZES), AXES)
    spec = P(("zh", "zl", "ylo"), ("x", "yhi", "core"))
    return jax.shard_map(
        per_device, mesh=fine, in_specs=(spec,), out_specs=spec, check_vma=False
    )
```

```python
import jax
import jax.numpy as jnp
from jax import lax
from jax.sharding import Mesh, PartitionSpec as P

AXES = ("zh", "zl", "ylo", "x", "yhi", "core")
SIZES = (4, 4, 2, 4, 2, 2)
LINE = ("zh", "zl")
PLANE = ("ylo", "x", "yhi")
SWAP = ((0, 1), (1, 0))
TURN = ((0, 0), (1, 2), (2, 1), (3, 3))
CROSS = ((0, 2), (1, 0), (2, 3), (3, 1))


def share(piece, size):
    copies = jnp.broadcast_to(piece[None], (size,) + piece.shape)
    return lax.all_to_all(copies, PLANE, 0, 0)


def along(piece, shift, shift_of_core_1=None):
    size = lax.axis_size(LINE)
    shifts = (shift, shift if shift_of_core_1 is None else shift_of_core_1)
    pairs = [
        (2 * place + core, 2 * ((place + shifts[core]) % size) + core)
        for place in range(size)
        for core in range(2)
    ]
    return lax.ppermute(piece, LINE + ("core",), pairs)


def onward(piece):
    return along(piece, 1, -1)


def launch(piece, side):
    size = lax.axis_size(LINE)
    pairs = []
    for place in range(size):
        for ylo in range(2):
            for core in range(2):
                to = ylo ^ side
                ahead = (place + 1 - 2 * to) % size
                pairs.append(
                    (
                        4 * place + 2 * ylo + core,
                        4 * ahead + 2 * (core ^ side) + to,
                    )
                )
    return lax.ppermute(piece, LINE + ("ylo", "core"), pairs)


def swap(pieces):
    return list(lax.ppermute(jnp.stack(pieces), "core", SWAP))


def put(blocks, block, place):
    return lax.dynamic_update_index_in_dim(blocks, block, place, 0)


def split(value):
    terms = []
    for _ in range(3):
        terms.append(lax.reduce_precision(value, 8, 7))
        value = value - terms[-1]
    return jnp.stack(terms)


def mix(left, right):
    return lax.dot_general(
        left, right, (((0, 2), (0, 1)), ((), ())), preferred_element_type=jnp.float32
    )


def per_device(iterate):
    rounded = iterate.astype(jnp.bfloat16)
    rows, cols = rounded.shape
    groups, steps = lax.axis_size("zh"), lax.axis_size("zl")
    chips = lax.axis_size(PLANE)
    total_cols = cols * chips
    own = lax.ppermute(rounded, ("ylo", "core"), TURN)
    other = lax.ppermute(own, "core", SWAP)
    slabs = groups * steps
    near, far = [own, launch(rounded, 0)], [None, launch(lax.ppermute(rounded, "core", SWAP), 1)]
    for step in range(2, slabs // 2):
        near.append(onward(near[-1]))
        far.append(onward(far[-1]))
    near.append(onward(near[-1]))
    back = [None] + swap(far[1:4]) + swap(far[4:6]) + swap(far[6:])
    slab, toward = lax.axis_index(LINE), 1 - 2 * lax.axis_index("core")
    half = jnp.zeros((slabs, rows, cols), jnp.bfloat16)
    for step in range(slabs // 2 + 1):
        half = put(half, near[step], (slab - step * toward) % slabs)
        if 0 < step < slabs // 2:
            half = put(half, back[step], (slab + step * toward) % slabs)
    partial_gram = lax.dot_general(
        jnp.concatenate([own, other], 0),
        half,
        (((1,), (2,)), ((), ())),
        preferred_element_type=jnp.float32,
    )
    partial_gram = partial_gram.transpose(1, 0, 2).astype(jnp.bfloat16)
    wide = own.astype(jnp.float32)
    extra = jnp.pad(split((wide * wide).sum(1)), ((0, 5), (0, 0)))
    extra = jnp.broadcast_to(extra.astype(jnp.bfloat16)[None], (chips, 8, rows))
    partial_gram = jnp.concatenate([partial_gram, extra], 1)
    met = lax.axis_index(PLANE) == lax.axis_index(LINE)
    residue = lax.axis_index("zl")
    partial_gram, met, residue = lax.optimization_barrier((partial_gram, met, residue))
    summands = lax.all_to_all(partial_gram, PLANE, 0, 0)
    summands, own, half, met, residue = lax.optimization_barrier(
        (summands, own, half, met, residue)
    )
    gram = summands.astype(jnp.float32).sum(0) / total_cols
    diagonal = gram[2 * rows :].sum(0)
    gram = gram[: 2 * rows]
    place = lax.broadcasted_iota(jnp.int32, gram.shape, 0)
    place = place - lax.broadcasted_iota(jnp.int32, gram.shape, 1)
    gram = jnp.where((place == 0) & met, diagonal[None], gram)
    gram_low = gram.astype(jnp.bfloat16)
    panel = share(gram_low, chips).reshape(groups, steps, 2 * rows, rows)
    here = lax.all_gather(gram_low, "zh", axis=0)
    panel, _ = lax.optimization_barrier((panel, here))
    right = (
        here,
        along(here, -2, 2),
        along(here, -1),
        along(here, 1),
    )
    left_own = [
        lax.dynamic_index_in_dim(panel, (residue + shift) % steps, 1, False)
        for shift in (0, 2, 1, steps - 1)
    ]
    left_other = lax.ppermute(jnp.stack(left_own), "core", SWAP)
    left_other = jnp.concatenate(
        [left_other[:, :, rows:], left_other[:, :, :rows]], 2
    )
    square = 0.0
    for place in range(steps):
        square = square + mix(left_own[place], right[place][:, :rows])
        square = lax.optimization_barrier(square)
    for place in range(steps):
        square = square + mix(left_other[place], right[place][:, rows:])
        square = lax.optimization_barrier(square)
    poly = (-4.775 * gram + 2.0315 * square).astype(jnp.bfloat16)
    panel = share(poly, chips)
    away = mix(panel[:, rows:], half).astype(jnp.bfloat16)
    away = lax.ppermute(away, ("ylo", "core"), CROSS)
    stay = mix(panel[:, :rows], half) + 3.4445 * own.astype(jnp.float32)
    stay = lax.ppermute(stay.astype(jnp.bfloat16), ("ylo", "core"), TURN)
    return stay.astype(jnp.float32) + away.astype(jnp.float32)


def solution(mesh):
    fine = Mesh(mesh.devices.reshape(SIZES), AXES)
    spec = P(("zh", "zl", "ylo"), ("x", "yhi", "core"))
    return jax.shard_map(
        per_device, mesh=fine, in_specs=(spec,), out_specs=spec, check_vma=False
    )
```

```python
import jax
import jax.numpy as jnp
from jax import lax
from jax.sharding import Mesh, PartitionSpec as P

AXES = ("zh", "zl", "ylo", "x", "yhi", "core")
SIZES = (4, 4, 2, 4, 2, 2)
LINE = ("zh", "zl")
PLANE = ("ylo", "yhi", "x")
SWAP = ((0, 1), (1, 0))
TURN = ((0, 0), (1, 2), (2, 1), (3, 3))
CROSS = ((0, 2), (1, 0), (2, 3), (3, 1))


def share(piece, size):
    copies = jnp.broadcast_to(piece[None], (size,) + piece.shape)
    return lax.all_to_all(copies, PLANE, 0, 0)


def along(piece, shift, shift_of_core_1=None):
    size = lax.axis_size(LINE)
    shifts = (shift, shift if shift_of_core_1 is None else shift_of_core_1)
    pairs = [
        (2 * place + core, 2 * ((place + shifts[core]) % size) + core)
        for place in range(size)
        for core in range(2)
    ]
    return lax.ppermute(piece, LINE + ("core",), pairs)


def onward(piece):
    return along(piece, 1, -1)


def launch(piece, side):
    size = lax.axis_size(LINE)
    pairs = []
    for place in range(size):
        for ylo in range(2):
            for core in range(2):
                to = ylo ^ side
                ahead = (place + 1 - 2 * to) % size
                pairs.append(
                    (
                        4 * place + 2 * ylo + core,
                        4 * ahead + 2 * (core ^ side) + to,
                    )
                )
    return lax.ppermute(piece, LINE + ("ylo", "core"), pairs)


def swap(pieces):
    return list(lax.ppermute(jnp.stack(pieces), "core", SWAP))


def put(blocks, block, place):
    return lax.dynamic_update_index_in_dim(blocks, block, place, 0)


def split(value):
    terms = []
    for _ in range(3):
        terms.append(lax.reduce_precision(value, 8, 7))
        value = value - terms[-1]
    return jnp.stack(terms)


def mix(left, right):
    return lax.dot_general(
        left, right, (((0, 2), (0, 1)), ((), ())), preferred_element_type=jnp.float32
    )


def per_device(iterate):
    rounded = iterate.astype(jnp.bfloat16)
    rows, cols = rounded.shape
    groups, steps = lax.axis_size("zh"), lax.axis_size("zl")
    chips = lax.axis_size(PLANE)
    total_cols = cols * chips
    own = lax.ppermute(rounded, ("ylo", "core"), TURN)
    other = lax.ppermute(own, "core", SWAP)
    slabs = groups * steps
    near, far = [own, launch(rounded, 0)], [None, launch(lax.ppermute(rounded, "core", SWAP), 1)]
    for step in range(2, slabs // 2):
        near.append(onward(near[-1]))
        far.append(onward(far[-1]))
    near.append(onward(near[-1]))
    back = [None] + swap(far[1:4]) + swap(far[4:6]) + swap(far[6:])
    slab, toward = lax.axis_index(LINE), 1 - 2 * lax.axis_index("core")
    half = jnp.zeros((slabs, rows, cols), jnp.bfloat16)
    for step in range(slabs // 2 + 1):
        half = put(half, near[step], (slab - step * toward) % slabs)
        if 0 < step < slabs // 2:
            half = put(half, back[step], (slab + step * toward) % slabs)
    partial_gram = lax.dot_general(
        jnp.concatenate([own, other], 0),
        half,
        (((1,), (2,)), ((), ())),
        preferred_element_type=jnp.float32,
    )
    partial_gram = partial_gram.transpose(1, 0, 2).astype(jnp.bfloat16)
    wide = own.astype(jnp.float32)
    extra = jnp.pad(split((wide * wide).sum(1)), ((0, 5), (0, 0)))
    extra = jnp.broadcast_to(extra.astype(jnp.bfloat16)[None], (chips, 8, rows))
    partial_gram = jnp.concatenate([partial_gram, extra], 1)
    met = lax.axis_index(PLANE) == lax.axis_index(LINE)
    residue = lax.axis_index("zl")
    partial_gram, met, residue = lax.optimization_barrier((partial_gram, met, residue))
    summands = lax.all_to_all(partial_gram, PLANE, 0, 0)
    summands, own, half, met, residue = lax.optimization_barrier(
        (summands, own, half, met, residue)
    )
    gram = summands.astype(jnp.float32).sum(0) / total_cols
    diagonal = gram[2 * rows :].sum(0)
    gram = gram[: 2 * rows]
    place = lax.broadcasted_iota(jnp.int32, gram.shape, 0)
    place = place - lax.broadcasted_iota(jnp.int32, gram.shape, 1)
    gram = jnp.where((place == 0) & met, diagonal[None], gram)
    gram_low = gram.astype(jnp.bfloat16)
    panel = share(gram_low, chips).reshape(groups, steps, 2 * rows, rows)
    here = lax.all_gather(gram_low, "zh", axis=0)
    panel, _ = lax.optimization_barrier((panel, here))
    right = (
        here,
        along(here, -2, 2),
        along(here, -1),
        along(here, 1),
    )
    left_own = [
        lax.dynamic_index_in_dim(panel, (residue + shift) % steps, 1, False)
        for shift in (0, 2, 1, steps - 1)
    ]
    left_other = swap(left_own[:2]) + swap(left_own[2:])
    left_other = [
        jnp.concatenate([part[:, rows:], part[:, :rows]], 1) for part in left_other
    ]
    square = 0.0
    for place in range(steps):
        square = square + mix(left_own[place], right[place][:, :rows])
        square = lax.optimization_barrier(square)
    for place in range(steps):
        square = square + mix(left_other[place], right[place][:, rows:])
        square = lax.optimization_barrier(square)
    poly = (-4.775 * gram + 2.0315 * square).astype(jnp.bfloat16)
    panel = share(poly, chips)
    away = mix(panel[:, rows:], half).astype(jnp.bfloat16)
    away = lax.ppermute(away, ("ylo", "core"), CROSS)
    stay = mix(panel[:, :rows], half) + 3.4445 * own.astype(jnp.float32)
    stay = lax.ppermute(stay.astype(jnp.bfloat16), ("ylo", "core"), TURN)
    return stay.astype(jnp.float32) + away.astype(jnp.float32)


def solution(mesh):
    fine = Mesh(mesh.devices.reshape(SIZES), AXES)
    spec = P(("zh", "zl", "ylo"), ("x", "yhi", "core"))
    return jax.shard_map(
        per_device, mesh=fine, in_specs=(spec,), out_specs=spec, check_vma=False
    )
```

```python
import jax
import jax.numpy as jnp
from jax import lax
from jax.sharding import Mesh, PartitionSpec as P

AXES = ("zh", "zl", "ylo", "x", "yhi", "core")
SIZES = (4, 4, 2, 4, 2, 2)
LINE = ("zh", "zl")
PLANE = ("ylo", "yhi", "x")
SWAP = ((0, 1), (1, 0))
TURN = ((0, 0), (1, 2), (2, 1), (3, 3))
CROSS = ((0, 2), (1, 0), (2, 3), (3, 1))


def share(piece, size):
    copies = jnp.broadcast_to(piece[None], (size,) + piece.shape)
    return lax.all_to_all(copies, PLANE, 0, 0)


def along(piece, shift, shift_of_core_1=None):
    size = lax.axis_size(LINE)
    shifts = (shift, shift if shift_of_core_1 is None else shift_of_core_1)
    pairs = [
        (2 * place + core, 2 * ((place + shifts[core]) % size) + core)
        for place in range(size)
        for core in range(2)
    ]
    return lax.ppermute(piece, LINE + ("core",), pairs)


def onward(piece):
    return along(piece, 1, -1)


def launch(piece, side):
    size = lax.axis_size(LINE)
    pairs = []
    for place in range(size):
        for ylo in range(2):
            for core in range(2):
                to = ylo ^ side
                ahead = (place + 1 - 2 * to) % size
                pairs.append(
                    (
                        4 * place + 2 * ylo + core,
                        4 * ahead + 2 * (core ^ side) + to,
                    )
                )
    return lax.ppermute(piece, LINE + ("ylo", "core"), pairs)


def swap(pieces):
    return list(lax.ppermute(jnp.stack(pieces), "core", SWAP))


def put(blocks, block, place):
    return lax.dynamic_update_index_in_dim(blocks, block, place, 0)


def split(value):
    terms = []
    for _ in range(3):
        terms.append(lax.reduce_precision(value, 8, 7))
        value = value - terms[-1]
    return jnp.stack(terms)


def mix(left, right):
    return lax.dot_general(
        left, right, (((0, 2), (0, 1)), ((), ())), preferred_element_type=jnp.float32
    )


def per_device(iterate):
    rounded = iterate.astype(jnp.bfloat16)
    rows, cols = rounded.shape
    groups, steps = lax.axis_size("zh"), lax.axis_size("zl")
    chips = lax.axis_size(PLANE)
    total_cols = cols * chips
    own = lax.ppermute(rounded, ("ylo", "core"), TURN)
    other = lax.ppermute(own, "core", SWAP)
    slabs = groups * steps
    near, far = [own, launch(rounded, 0)], [None, launch(lax.ppermute(rounded, "core", SWAP), 1)]
    for step in range(2, slabs // 2):
        near.append(onward(near[-1]))
        far.append(onward(far[-1]))
    near.append(onward(near[-1]))
    back = [None] + swap(far[1:4]) + swap(far[4:6]) + swap(far[6:])
    slab, toward = lax.axis_index(LINE), 1 - 2 * lax.axis_index("core")
    half = jnp.zeros((slabs, rows, cols), jnp.bfloat16)
    for step in range(slabs // 2 + 1):
        half = put(half, near[step], (slab - step * toward) % slabs)
        if 0 < step < slabs // 2:
            half = put(half, back[step], (slab + step * toward) % slabs)
    partial_gram = lax.dot_general(
        jnp.concatenate([own, other], 0),
        half,
        (((1,), (2,)), ((), ())),
        preferred_element_type=jnp.float32,
    )
    partial_gram = partial_gram.transpose(1, 0, 2).astype(jnp.bfloat16)
    wide = own.astype(jnp.float32)
    extra = jnp.pad(split((wide * wide).sum(1)), ((0, 5), (0, 0)))
    extra = jnp.broadcast_to(extra.astype(jnp.bfloat16)[None], (chips, 8, rows))
    partial_gram = jnp.concatenate([partial_gram, extra], 1)
    met = lax.axis_index(PLANE) == lax.axis_index(LINE)
    residue = lax.axis_index("zl")
    partial_gram, met, residue = lax.optimization_barrier((partial_gram, met, residue))
    summands = lax.all_to_all(partial_gram, PLANE, 0, 0)
    summands, own, half, met, residue = lax.optimization_barrier(
        (summands, own, half, met, residue)
    )
    gram = summands.astype(jnp.float32).sum(0) / total_cols
    diagonal = gram[2 * rows :].sum(0)
    gram = gram[: 2 * rows]
    place = lax.broadcasted_iota(jnp.int32, gram.shape, 0)
    place = place - lax.broadcasted_iota(jnp.int32, gram.shape, 1)
    gram = jnp.where((place == 0) & met, diagonal[None], gram)
    gram_low = gram.astype(jnp.bfloat16)
    panel = share(gram_low, chips).reshape(groups, steps, 2 * rows, rows)
    here = lax.all_gather(gram_low, "zh", axis=0)
    panel, _ = lax.optimization_barrier((panel, here))
    right = (
        here,
        along(here, -1),
        along(here, 1),
        along(here, -2, 2),
    )
    left_own = [
        lax.dynamic_index_in_dim(panel, (residue + shift) % steps, 1, False)
        for shift in (0, 1, steps - 1, 2)
    ]
    left_other = swap(left_own[:2]) + swap(left_own[2:])
    left_other = [
        jnp.concatenate([part[:, rows:], part[:, :rows]], 1) for part in left_other
    ]
    square = 0.0
    for place in range(steps):
        square = square + mix(left_own[place], right[place][:, :rows])
        square = lax.optimization_barrier(square)
    for place in range(steps):
        square = square + mix(left_other[place], right[place][:, rows:])
        square = lax.optimization_barrier(square)
    poly = (-4.775 * gram + 2.0315 * square).astype(jnp.bfloat16)
    panel = share(poly, chips)
    away = mix(panel[:, rows:], half).astype(jnp.bfloat16)
    away = lax.ppermute(away, ("ylo", "core"), CROSS)
    stay = mix(panel[:, :rows], half) + 3.4445 * own.astype(jnp.float32)
    stay = lax.ppermute(stay.astype(jnp.bfloat16), ("ylo", "core"), TURN)
    return stay.astype(jnp.float32) + away.astype(jnp.float32)


def solution(mesh):
    fine = Mesh(mesh.devices.reshape(SIZES), AXES)
    spec = P(("zh", "zl", "ylo"), ("x", "yhi", "core"))
    return jax.shard_map(
        per_device, mesh=fine, in_specs=(spec,), out_specs=spec, check_vma=False
    )
```

```python
import jax
import jax.numpy as jnp
from jax import lax
from jax.sharding import Mesh, PartitionSpec as P

AXES = ("zh", "zl", "ylo", "x", "yhi", "core")
SIZES = (4, 4, 2, 4, 2, 2)
LINE = ("zh", "zl")
PLANE = ("ylo", "yhi", "x")
SWAP = ((0, 1), (1, 0))
TURN = ((0, 0), (1, 2), (2, 1), (3, 3))
CROSS = ((0, 2), (1, 0), (2, 3), (3, 1))


def share(piece, size):
    copies = jnp.broadcast_to(piece[None], (size,) + piece.shape)
    return lax.all_to_all(copies, PLANE, 0, 0)


def along(piece, shift, shift_of_core_1=None):
    size = lax.axis_size(LINE)
    shifts = (shift, shift if shift_of_core_1 is None else shift_of_core_1)
    pairs = [
        (2 * place + core, 2 * ((place + shifts[core]) % size) + core)
        for place in range(size)
        for core in range(2)
    ]
    return lax.ppermute(piece, LINE + ("core",), pairs)


def onward(piece):
    return along(piece, 1, -1)


def launch(piece, side):
    size = lax.axis_size(LINE)
    pairs = []
    for place in range(size):
        for ylo in range(2):
            for core in range(2):
                to = ylo ^ side
                ahead = (place + 1 - 2 * to) % size
                pairs.append(
                    (
                        4 * place + 2 * ylo + core,
                        4 * ahead + 2 * (core ^ side) + to,
                    )
                )
    return lax.ppermute(piece, LINE + ("ylo", "core"), pairs)


def swap(pieces):
    return list(lax.ppermute(jnp.stack(pieces), "core", SWAP))


def put(blocks, block, place):
    return lax.dynamic_update_index_in_dim(blocks, block, place, 0)


def split(value):
    terms = []
    for _ in range(3):
        terms.append(lax.reduce_precision(value, 8, 7))
        value = value - terms[-1]
    return jnp.stack(terms)


def mix(left, right):
    return lax.dot_general(
        left, right, (((0, 2), (0, 1)), ((), ())), preferred_element_type=jnp.float32
    )


def per_device(iterate):
    rounded = iterate.astype(jnp.bfloat16)
    rows, cols = rounded.shape
    groups, steps = lax.axis_size("zh"), lax.axis_size("zl")
    chips = lax.axis_size(PLANE)
    total_cols = cols * chips
    slabs = groups * steps
    near = [None, launch(rounded, 0)]
    far = [None, launch(lax.ppermute(rounded, "core", SWAP), 1)]
    for step in range(2, slabs // 2 + 1):
        if step == 4:
            late, far[-1] = lax.optimization_barrier((rounded, far[-1]))
            own = lax.ppermute(late, ("ylo", "core"), TURN)
        near.append(onward(near[-1]))
        if step < slabs // 2:
            far.append(onward(far[-1]))
    other = lax.ppermute(own, "core", SWAP)
    back = [None] + swap(far[1:4]) + swap(far[4:6]) + swap(far[6:])
    slab, toward = lax.axis_index(LINE), 1 - 2 * lax.axis_index("core")
    half = jnp.zeros((slabs, rows, cols), jnp.bfloat16)
    for step in range(1, slabs // 2 + 1):
        half = put(half, near[step], (slab - step * toward) % slabs)
        if step < slabs // 2:
            half = put(half, back[step], (slab + step * toward) % slabs)
    half = put(half, own, slab)
    partial_gram = lax.dot_general(
        jnp.concatenate([own, other], 0),
        half,
        (((1,), (2,)), ((), ())),
        preferred_element_type=jnp.float32,
    )
    partial_gram = partial_gram.transpose(1, 0, 2).astype(jnp.bfloat16)
    wide = own.astype(jnp.float32)
    extra = jnp.pad(split((wide * wide).sum(1)), ((0, 5), (0, 0)))
    extra = jnp.broadcast_to(extra.astype(jnp.bfloat16)[None], (chips, 8, rows))
    partial_gram = jnp.concatenate([partial_gram, extra], 1)
    met = lax.axis_index(PLANE) == lax.axis_index(LINE)
    residue = lax.axis_index("zl")
    partial_gram, met, residue = lax.optimization_barrier((partial_gram, met, residue))
    summands = lax.all_to_all(partial_gram, PLANE, 0, 0)
    summands, own, half, met, residue = lax.optimization_barrier(
        (summands, own, half, met, residue)
    )
    gram = summands.astype(jnp.float32).sum(0) / total_cols
    diagonal = gram[2 * rows :].sum(0)
    gram = gram[: 2 * rows]
    place = lax.broadcasted_iota(jnp.int32, gram.shape, 0)
    place = place - lax.broadcasted_iota(jnp.int32, gram.shape, 1)
    gram = jnp.where((place == 0) & met, diagonal[None], gram)
    gram_low = gram.astype(jnp.bfloat16)
    panel = share(gram_low, chips).reshape(groups, steps, 2 * rows, rows)
    here = lax.all_gather(gram_low, "zh", axis=0)
    panel, _ = lax.optimization_barrier((panel, here))
    right = (
        here,
        along(here, -1),
        along(here, 1),
        along(here, -2, 2),
    )
    left_own = [
        lax.dynamic_index_in_dim(panel, (residue + shift) % steps, 1, False)
        for shift in (0, 1, steps - 1, 2)
    ]
    left_other = swap(left_own[:2]) + swap(left_own[2:])
    left_other = [
        jnp.concatenate([part[:, rows:], part[:, :rows]], 1) for part in left_other
    ]
    square = 0.0
    for place in range(steps):
        square = square + mix(left_own[place], right[place][:, :rows])
        square = lax.optimization_barrier(square)
    for place in range(steps):
        square = square + mix(left_other[place], right[place][:, rows:])
        square = lax.optimization_barrier(square)
    poly = (-4.775 * gram + 2.0315 * square).astype(jnp.bfloat16)
    panel = share(poly, chips)
    away = mix(panel[:, rows:], half).astype(jnp.bfloat16)
    away = lax.ppermute(away, ("ylo", "core"), CROSS)
    stay = mix(panel[:, :rows], half) + 3.4445 * own.astype(jnp.float32)
    stay = lax.ppermute(stay.astype(jnp.bfloat16), ("ylo", "core"), TURN)
    return stay.astype(jnp.float32) + away.astype(jnp.float32)


def solution(mesh):
    fine = Mesh(mesh.devices.reshape(SIZES), AXES)
    spec = P(("zh", "zl", "ylo"), ("x", "yhi", "core"))
    return jax.shard_map(
        per_device, mesh=fine, in_specs=(spec,), out_specs=spec, check_vma=False
    )
```

```python
import jax
import jax.numpy as jnp
from jax import lax
from jax.sharding import Mesh, PartitionSpec as P

AXES = ("zh", "zl", "ylo", "x", "yhi", "core")
SIZES = (4, 4, 2, 4, 2, 2)
LINE = ("zh", "zl")
PLANE = ("ylo", "yhi", "x")
SWAP = ((0, 1), (1, 0))
TURN = ((0, 0), (1, 2), (2, 1), (3, 3))
CROSS = ((0, 2), (1, 0), (2, 3), (3, 1))


def share(piece, size):
    copies = jnp.broadcast_to(piece[None], (size,) + piece.shape)
    return lax.all_to_all(copies, PLANE, 0, 0)


def along(piece, shift, shift_of_core_1=None):
    size = lax.axis_size(LINE)
    shifts = (shift, shift if shift_of_core_1 is None else shift_of_core_1)
    pairs = [
        (2 * place + core, 2 * ((place + shifts[core]) % size) + core)
        for place in range(size)
        for core in range(2)
    ]
    return lax.ppermute(piece, LINE + ("core",), pairs)


def onward(piece):
    return along(piece, 1, -1)


def launch(piece, side):
    size = lax.axis_size(LINE)
    pairs = []
    for place in range(size):
        for ylo in range(2):
            for core in range(2):
                to = ylo ^ side
                ahead = (place + 1 - 2 * to) % size
                pairs.append(
                    (
                        4 * place + 2 * ylo + core,
                        4 * ahead + 2 * (core ^ side) + to,
                    )
                )
    return lax.ppermute(piece, LINE + ("ylo", "core"), pairs)


def swap(pieces):
    return list(lax.ppermute(jnp.stack(pieces), "core", SWAP))


def put(blocks, block, place):
    return lax.dynamic_update_index_in_dim(blocks, block, place, 0)


def split(value):
    terms = []
    for _ in range(3):
        terms.append(lax.reduce_precision(value, 8, 7))
        value = value - terms[-1]
    return jnp.stack(terms)


def mix(left, right):
    return lax.dot_general(
        left, right, (((0, 2), (0, 1)), ((), ())), preferred_element_type=jnp.float32
    )


def per_device(iterate):
    rounded = iterate.astype(jnp.bfloat16)
    rows, cols = rounded.shape
    groups, steps = lax.axis_size("zh"), lax.axis_size("zl")
    chips = lax.axis_size(PLANE)
    total_cols = cols * chips
    own = lax.ppermute(rounded, ("ylo", "core"), TURN)
    other = lax.ppermute(own, "core", SWAP)
    slabs = groups * steps
    near, far = [own, launch(rounded, 0)], [None, launch(lax.ppermute(rounded, "core", SWAP), 1)]
    for step in range(2, slabs // 2):
        near.append(onward(near[-1]))
        far.append(onward(far[-1]))
    near.append(onward(near[-1]))
    back = [None] + swap(far[1:4]) + swap(far[4:6]) + swap(far[6:])
    slab, toward = lax.axis_index(LINE), 1 - 2 * lax.axis_index("core")
    half = jnp.zeros((slabs, rows, cols), jnp.bfloat16)
    for step in range(slabs // 2 + 1):
        half = put(half, near[step], (slab - step * toward) % slabs)
        if 0 < step < slabs // 2:
            half = put(half, back[step], (slab + step * toward) % slabs)
    partial_gram = lax.dot_general(
        jnp.concatenate([own, other], 0),
        half,
        (((1,), (2,)), ((), ())),
        preferred_element_type=jnp.float32,
    )
    partial_gram = partial_gram.transpose(1, 0, 2).astype(jnp.bfloat16)
    wide = own.astype(jnp.float32)
    extra = jnp.pad(split((wide * wide).sum(1)), ((0, 5), (0, 0)))
    extra = jnp.broadcast_to(extra.astype(jnp.bfloat16)[None], (chips, 8, rows))
    partial_gram = jnp.concatenate([partial_gram, extra], 1)
    met = lax.axis_index(PLANE) == lax.axis_index(LINE)
    residue = lax.axis_index("zl")
    partial_gram, met, residue = lax.optimization_barrier((partial_gram, met, residue))
    summands = lax.all_to_all(partial_gram, PLANE, 0, 0)
    summands, own, half, met, residue = lax.optimization_barrier(
        (summands, own, half, met, residue)
    )
    gram = summands.astype(jnp.float32).sum(0) / total_cols
    diagonal = gram[2 * rows :].sum(0)
    gram = gram[: 2 * rows]
    place = lax.broadcasted_iota(jnp.int32, gram.shape, 0)
    place = place - lax.broadcasted_iota(jnp.int32, gram.shape, 1)
    gram = jnp.where((place == 0) & met, diagonal[None], gram)
    gram_low = gram.astype(jnp.bfloat16)
    panel = share(gram_low, chips).reshape(groups, steps, 2 * rows, rows)
    here = lax.all_gather(gram_low, "zh", axis=0)
    panel, _ = lax.optimization_barrier((panel, here))
    right = (
        here,
        along(here, -2, 2),
        along(here, -1),
        along(here, 1),
    )
    left_own = [
        lax.dynamic_index_in_dim(panel, (residue + shift) % steps, 1, False)
        for shift in (0, 2, 1, steps - 1)
    ]
    left_other = swap(left_own[:2]) + swap(left_own[2:])
    left_other = [
        jnp.concatenate([part[:, rows:], part[:, :rows]], 1) for part in left_other
    ]
    square = 0.0
    for place in range(steps):
        square = square + mix(left_own[place], right[place][:, :rows])
        square = lax.optimization_barrier(square)
    for place in range(steps):
        square = square + mix(left_other[place], right[place][:, rows:])
        square = lax.optimization_barrier(square)
    poly = (-4.775 * gram + 2.0315 * square).astype(jnp.bfloat16)
    poly, own = lax.optimization_barrier((poly, own))
    panel = share(poly, chips)
    scaled = lax.optimization_barrier(3.4445 * own.astype(jnp.float32))
    away = mix(panel[:, rows:], half).astype(jnp.bfloat16)
    away = lax.ppermute(away, ("ylo", "core"), CROSS)
    stay = mix(panel[:, :rows], half) + scaled
    stay = lax.ppermute(stay.astype(jnp.bfloat16), ("ylo", "core"), TURN)
    return stay.astype(jnp.float32) + away.astype(jnp.float32)


def solution(mesh):
    fine = Mesh(mesh.devices.reshape(SIZES), AXES)
    spec = P(("zh", "zl", "ylo"), ("x", "yhi", "core"))
    return jax.shard_map(
        per_device, mesh=fine, in_specs=(spec,), out_specs=spec, check_vma=False
    )
```

```python
import jax
import jax.numpy as jnp
from jax import lax
from jax.sharding import Mesh, PartitionSpec as P

AXES = ("zh", "zl", "ylo", "x", "yhi", "core")
SIZES = (4, 4, 2, 4, 2, 2)
LINE = ("zh", "zl")
PLANE = ("ylo", "yhi", "x")
SWAP = ((0, 1), (1, 0))
TURN = ((0, 0), (1, 2), (2, 1), (3, 3))
CROSS = ((0, 2), (1, 0), (2, 3), (3, 1))


def share(piece, size):
    copies = jnp.broadcast_to(piece[None], (size,) + piece.shape)
    return lax.all_to_all(copies, PLANE, 0, 0)


def along(piece, shift, shift_of_core_1=None):
    size = lax.axis_size(LINE)
    shifts = (shift, shift if shift_of_core_1 is None else shift_of_core_1)
    pairs = [
        (2 * place + core, 2 * ((place + shifts[core]) % size) + core)
        for place in range(size)
        for core in range(2)
    ]
    return lax.ppermute(piece, LINE + ("core",), pairs)


def onward(piece):
    return along(piece, 1, -1)


def launch(piece, side):
    size = lax.axis_size(LINE)
    pairs = []
    for place in range(size):
        for ylo in range(2):
            for core in range(2):
                to = ylo ^ side
                ahead = (place + 1 - 2 * to) % size
                pairs.append(
                    (
                        4 * place + 2 * ylo + core,
                        4 * ahead + 2 * (core ^ side) + to,
                    )
                )
    return lax.ppermute(piece, LINE + ("ylo", "core"), pairs)


def swap(pieces):
    return list(lax.ppermute(jnp.stack(pieces), "core", SWAP))


def put(blocks, block, place):
    return lax.dynamic_update_index_in_dim(blocks, block, place, 0)


def split(value):
    terms = []
    for _ in range(3):
        terms.append(lax.reduce_precision(value, 8, 7))
        value = value - terms[-1]
    return jnp.stack(terms)


def mix(left, right):
    return lax.dot_general(
        left, right, (((0, 2), (0, 1)), ((), ())), preferred_element_type=jnp.float32
    )


def per_device(iterate):
    rounded = iterate.astype(jnp.bfloat16)
    rows, cols = rounded.shape
    groups, steps = lax.axis_size("zh"), lax.axis_size("zl")
    chips = lax.axis_size(PLANE)
    total_cols = cols * chips
    own = lax.ppermute(rounded, ("ylo", "core"), TURN)
    other = lax.ppermute(own, "core", SWAP)
    slabs = groups * steps
    near, far = [own, launch(rounded, 0)], [None, launch(lax.ppermute(rounded, "core", SWAP), 1)]
    for step in range(2, slabs // 2):
        near.append(onward(near[-1]))
        far.append(onward(far[-1]))
    near.append(onward(near[-1]))
    back = [None] + swap(far[1:4]) + swap(far[4:6]) + swap(far[6:])
    slab, toward = lax.axis_index(LINE), 1 - 2 * lax.axis_index("core")
    half = jnp.zeros((slabs, rows, cols), jnp.bfloat16)
    for step in range(slabs // 2 + 1):
        half = put(half, near[step], (slab - step * toward) % slabs)
        if 0 < step < slabs // 2:
            half = put(half, back[step], (slab + step * toward) % slabs)
    partial_gram = lax.dot_general(
        jnp.concatenate([own, other], 0),
        half,
        (((1,), (2,)), ((), ())),
        preferred_element_type=jnp.float32,
    )
    partial_gram = partial_gram.transpose(1, 0, 2).astype(jnp.bfloat16)
    wide = own.astype(jnp.float32)
    extra = jnp.pad(split((wide * wide).sum(1)), ((0, 5), (0, 0)))
    extra = jnp.broadcast_to(extra.astype(jnp.bfloat16)[None], (chips, 8, rows))
    partial_gram = jnp.concatenate([partial_gram, extra], 1)
    met = lax.axis_index(PLANE) == lax.axis_index(LINE)
    residue = lax.axis_index("zl")
    partial_gram, met, residue = lax.optimization_barrier((partial_gram, met, residue))
    summands = lax.all_to_all(partial_gram, PLANE, 0, 0)
    summands, own, half, met, residue = lax.optimization_barrier(
        (summands, own, half, met, residue)
    )
    gram = summands.astype(jnp.float32).sum(0) / total_cols
    diagonal = gram[2 * rows :].sum(0)
    gram = gram[: 2 * rows]
    place = lax.broadcasted_iota(jnp.int32, gram.shape, 0)
    place = place - lax.broadcasted_iota(jnp.int32, gram.shape, 1)
    gram = jnp.where((place == 0) & met, diagonal[None], gram)
    gram_low = gram.astype(jnp.bfloat16)
    panel = share(gram_low, chips).reshape(groups, steps, 2 * rows, rows)
    here = lax.all_gather(gram_low, "zh", axis=0)
    panel, _ = lax.optimization_barrier((panel, here))
    right = (
        here,
        along(here, -2, 2),
        along(here, -1),
        along(here, 1),
    )
    left_own = [
        lax.dynamic_index_in_dim(panel, (residue + shift) % steps, 1, False)
        for shift in (0, 2, 1, steps - 1)
    ]
    left_other = swap(left_own[:2]) + swap(left_own[2:])
    left_other = [
        jnp.concatenate([part[:, rows:], part[:, :rows]], 1) for part in left_other
    ]
    square = 0.0
    for place in range(steps):
        square = square + mix(left_own[place], right[place][:, :rows])
        square = lax.optimization_barrier(square)
    for place in range(steps):
        square = square + mix(left_other[place], right[place][:, rows:])
        square = lax.optimization_barrier(square)
    poly = (-4.775 * gram + 2.0315 * square).astype(jnp.bfloat16)
    panel = share(poly, chips)
    product = mix(panel, half)
    away = product[rows:].astype(jnp.bfloat16)
    away = lax.ppermute(away, ("ylo", "core"), CROSS)
    stay = product[:rows] + 3.4445 * own.astype(jnp.float32)
    stay = lax.ppermute(stay.astype(jnp.bfloat16), ("ylo", "core"), TURN)
    return stay.astype(jnp.float32) + away.astype(jnp.float32)


def solution(mesh):
    fine = Mesh(mesh.devices.reshape(SIZES), AXES)
    spec = P(("zh", "zl", "ylo"), ("x", "yhi", "core"))
    return jax.shard_map(
        per_device, mesh=fine, in_specs=(spec,), out_specs=spec, check_vma=False
    )
```

```python
import jax
import jax.numpy as jnp
from jax import lax
from jax.sharding import Mesh, PartitionSpec as P

AXES = ("zh", "zl", "ylo", "x", "yhi", "core")
SIZES = (4, 4, 2, 4, 2, 2)
LINE = ("zh", "zl")
PLANE = ("ylo", "yhi", "x")
SWAP = ((0, 1), (1, 0))
TURN = ((0, 0), (1, 2), (2, 1), (3, 3))
CROSS = ((0, 2), (1, 0), (2, 3), (3, 1))


def share(piece, size):
    copies = jnp.broadcast_to(piece[None], (size,) + piece.shape)
    return lax.all_to_all(copies, PLANE, 0, 0)


def along(piece, shift, shift_of_core_1=None):
    size = lax.axis_size(LINE)
    shifts = (shift, shift if shift_of_core_1 is None else shift_of_core_1)
    pairs = [
        (2 * place + core, 2 * ((place + shifts[core]) % size) + core)
        for place in range(size)
        for core in range(2)
    ]
    return lax.ppermute(piece, LINE + ("core",), pairs)


def onward(piece):
    return along(piece, 1, -1)


def launch(piece, side):
    size = lax.axis_size(LINE)
    pairs = []
    for place in range(size):
        for ylo in range(2):
            for core in range(2):
                to = ylo ^ side
                ahead = (place + 1 - 2 * to) % size
                pairs.append(
                    (
                        4 * place + 2 * ylo + core,
                        4 * ahead + 2 * (core ^ side) + to,
                    )
                )
    return lax.ppermute(piece, LINE + ("ylo", "core"), pairs)


def swap(pieces):
    return list(lax.ppermute(jnp.stack(pieces), "core", SWAP))


def put(blocks, block, place):
    return lax.dynamic_update_index_in_dim(blocks, block, place, 0)


def split(value):
    terms = []
    for _ in range(3):
        terms.append(lax.reduce_precision(value, 8, 7))
        value = value - terms[-1]
    return jnp.stack(terms)


def mix(left, right):
    return lax.dot_general(
        left, right, (((0, 2), (0, 1)), ((), ())), preferred_element_type=jnp.float32
    )


def per_device(iterate):
    rounded = iterate.astype(jnp.bfloat16)
    rows, cols = rounded.shape
    groups, steps = lax.axis_size("zh"), lax.axis_size("zl")
    chips = lax.axis_size(PLANE)
    total_cols = cols * chips
    own = lax.ppermute(rounded, ("ylo", "core"), TURN)
    other = lax.ppermute(own, "core", SWAP)
    slabs = groups * steps
    near, far = [own, launch(rounded, 0)], [None, launch(lax.ppermute(rounded, "core", SWAP), 1)]
    for step in range(2, slabs // 2):
        near.append(onward(near[-1]))
        far.append(onward(far[-1]))
    near.append(onward(near[-1]))
    back = [None] + swap(far[1:6]) + swap(far[6:])
    slab, toward = lax.axis_index(LINE), 1 - 2 * lax.axis_index("core")
    half = jnp.zeros((slabs, rows, cols), jnp.bfloat16)
    for step in range(slabs // 2 + 1):
        half = put(half, near[step], (slab - step * toward) % slabs)
        if 0 < step < slabs // 2:
            half = put(half, back[step], (slab + step * toward) % slabs)
    partial_gram = lax.dot_general(
        jnp.concatenate([own, other], 0),
        half,
        (((1,), (2,)), ((), ())),
        preferred_element_type=jnp.float32,
    )
    partial_gram = partial_gram.transpose(1, 0, 2).astype(jnp.bfloat16)
    wide = own.astype(jnp.float32)
    extra = jnp.pad(split((wide * wide).sum(1)), ((0, 5), (0, 0)))
    extra = jnp.broadcast_to(extra.astype(jnp.bfloat16)[None], (chips, 8, rows))
    partial_gram = jnp.concatenate([partial_gram, extra], 1)
    met = lax.axis_index(PLANE) == lax.axis_index(LINE)
    residue = lax.axis_index("zl")
    partial_gram, met, residue = lax.optimization_barrier((partial_gram, met, residue))
    summands = lax.all_to_all(partial_gram, PLANE, 0, 0)
    summands, own, half, met, residue = lax.optimization_barrier(
        (summands, own, half, met, residue)
    )
    gram = summands.astype(jnp.float32).sum(0) / total_cols
    diagonal = gram[2 * rows :].sum(0)
    gram = gram[: 2 * rows]
    place = lax.broadcasted_iota(jnp.int32, gram.shape, 0)
    place = place - lax.broadcasted_iota(jnp.int32, gram.shape, 1)
    gram = jnp.where((place == 0) & met, diagonal[None], gram)
    gram_low = gram.astype(jnp.bfloat16)
    panel = share(gram_low, chips).reshape(groups, steps, 2 * rows, rows)
    here = lax.all_gather(gram_low, "zh", axis=0)
    panel, _ = lax.optimization_barrier((panel, here))
    right = (
        here,
        along(here, -2, 2),
        along(here, -1),
        along(here, 1),
    )
    left_own = [
        lax.dynamic_index_in_dim(panel, (residue + shift) % steps, 1, False)
        for shift in (0, 2, 1, steps - 1)
    ]
    left_other = swap(left_own[:2]) + swap(left_own[2:])
    left_other = [
        jnp.concatenate([part[:, rows:], part[:, :rows]], 1) for part in left_other
    ]
    square = 0.0
    for place in range(steps):
        square = square + mix(left_own[place], right[place][:, :rows])
        square = lax.optimization_barrier(square)
    for place in range(steps):
        square = square + mix(left_other[place], right[place][:, rows:])
        square = lax.optimization_barrier(square)
    poly = (-4.775 * gram + 2.0315 * square).astype(jnp.bfloat16)
    panel = share(poly, chips)
    away = mix(panel[:, rows:], half).astype(jnp.bfloat16)
    away = lax.ppermute(away, ("ylo", "core"), CROSS)
    stay = mix(panel[:, :rows], half) + 3.4445 * own.astype(jnp.float32)
    stay = lax.ppermute(stay.astype(jnp.bfloat16), ("ylo", "core"), TURN)
    return stay.astype(jnp.float32) + away.astype(jnp.float32)


def solution(mesh):
    fine = Mesh(mesh.devices.reshape(SIZES), AXES)
    spec = P(("zh", "zl", "ylo"), ("x", "yhi", "core"))
    return jax.shard_map(
        per_device, mesh=fine, in_specs=(spec,), out_specs=spec, check_vma=False
    )
```
